128 devices in a mesh: section: 4 (over z), dp: 32 (over x, y, core).
Axes of the slice: x: 4, y: 4, z: 4, core: 2. Of those that a mesh axis runs over, the one named last changes fastest.
Arguments:
- tokens_in: bfloat16 [2, 192, 8192], P(None, None, 'dp'), may hold values from -6 to 6
- cotangent: bfloat16 [2, 192, 8192], P(None, None, 'dp'), may hold values from -6 to 6
- base_weight: bfloat16 [4, 8192, 8192], P('section', None, 'dp'), may hold values from -0.0625 to 0.0625
- norm_gain: bfloat16 [4, 8192], P('section', 'dp'), may hold values from 0.25 to 5.5, as said below
- adapter_a: bfloat16 [4, 64, 32, 8192], P('section', None, None, 'dp'), may hold values from -0.0625 to 0.0625
- adapter_b: bfloat16 [4, 64, 32, 8192], P('section', None, None, 'dp'), may hold values from -1 to 1
- seg_ids: int32 [2, 192], replicated, may hold values from 0 to 63, never falling along the last dimension, each value on 1 to 48 neighbouring positions
- live_counts: int32 [2, 64], replicated, may hold values from 1 to 48
Outputs:
- section_out: bfloat16 [4, 2, 192, 8192], P('section', None, None, 'dp')
- grad_a: float32 [4, 64, 32, 8192], P('section', None, None, 'dp')
- grad_b: float32 [4, 64, 32, 8192], P('section', None, None, 'dp')
The draws below stay inside these ranges and needn't reach their ends.
Inputs may be any that keep to these rules, and one draw needn't show every extreme that they name: `seg_ids`: never falling along the rows; every adapter has 1 to 48 rows in each micro-batch, and some adapter exactly 48. `norm_gain`: Positive.
All inputs are finite; a program needn't handle non-finite values.
Results may differ from the reference program's by a relative error of at most 0.018.
Values may be sent and summed in bfloat16 or wider, within the bound.
No kernel may reach another device: no remote copies, remote signals or barrier semaphores. Data moves between devices by JAX's collectives and lax.ppermute only.
A program may use at most 128 MiB of HBM per device.

```python
import math
import jax
import jax.numpy as jnp
import numpy as np
from jax import lax

D = 8192
RANK = 32
MICRO = 2
ADAPTERS = 64
ROWS = 192
LAYERS = 4
MOST = 48
N_DP = 32


def ramp_gain(key, lower, upper, jitter):
    place = jnp.arange(D, dtype=jnp.float32) / (D - 1)
    trend = jnp.exp(math.log(lower) + (math.log(upper) - math.log(lower)) * place)
    rough = jax.random.uniform(key, (LAYERS, D), jnp.float32, 1.0 - jitter, 1.0 + jitter)
    return (trend[None, :] * rough).astype(jnp.bfloat16)


def draw_norm_gain(key, part):
    key = jax.random.fold_in(key, 11)
    return ramp_gain(key, 0.5, 2.5, 0.2)


def touch_ends(drawn, own_key, least, top_value):
    dims = drawn.shape
    spot = [jax.random.randint(jax.random.fold_in(own_key, axis), (), 0, dims[axis]) for axis in range(len(dims))]
    drawn = drawn.at[tuple(spot)].set(least)
    longest = dims.index(max(dims))
    spot[longest] = (spot[longest] + 1) % dims[longest]
    return drawn.at[tuple(spot)].set(top_value)


def steps_of(rng, dims, shards, low, top_value):
    level, own = 1.0, jax.random.fold_in(rng, 6)
    for dim, shards_of in shards:
        heights = jnp.exp(jax.random.uniform(jax.random.fold_in(own, dim), (shards_of,), jnp.float32, low / len(shards), top_value / len(shards)))
        level = level * jnp.repeat(heights, dims[dim] // shards_of).reshape([-1 if axis == dim else 1 for axis in range(len(dims))])
    return level


def split_up(count, total, reach, slope):
    portions = [(1 << 20) // math.isqrt(standing ** slope) + 1 for standing in range(2, count + 1)]
    surplus, given = total - reach - (count - 1), [1] * (count - 1)
    while surplus > 0:
        movable = [i for i in range(count - 1) if given[i] < reach]
        whole, budget = sum([portions[i] for i in movable]), surplus
        for i in movable:
            addition = min(reach - given[i], max(1, budget * portions[i] // whole), surplus)
            given[i] = given[i] + addition
            surplus = surplus - addition
    return np.array([reach] + given)


def uneven_parts(own_key, amount, total, most, slope):
    if amount == 2:
        one = jax.random.randint(own_key, (), max(1, total - most), min(most, total - 1) + 1)
        return jnp.stack([one, total - one])
    tallies = jnp.asarray(split_up(amount, total, most, slope), jnp.int32)
    pairs = (amount - 1) // 2
    donor, receiver = tallies[1:1 + 2 * pairs:2], tallies[2:2 + 2 * pairs:2]
    slack = jnp.minimum(donor - 1, most - receiver)
    moved = jax.random.randint(jax.random.fold_in(own_key, 1), (pairs,), 0, 1 << 20) % (slack + 1)
    tallies = tallies.at[1:1 + 2 * pairs:2].set(donor - moved).at[2:2 + 2 * pairs:2].set(receiver + moved)
    return tallies[jax.random.permutation(jax.random.fold_in(own_key, 2), amount)]


def normal_values(key, extent, deviation, reach, cuts=(), kind=jnp.bfloat16):
    factor_of = steps_of(key, extent, cuts, -0.22, 0.18) if cuts else 1.0
    values = jax.random.normal(key, extent, jnp.float32) * deviation * factor_of
    return jnp.minimum(jnp.maximum(values, -reach), reach).astype(kind)


def setup_inputs(seed: int = 0) -> dict:
    streams_of = jax.random.split(jax.random.key(seed), 9)
    return {
        "tokens_in": normal_values(streams_of[0], (MICRO, ROWS, D), 1.0, 6.0, ((2, 32),)),
        "cotangent": normal_values(streams_of[1], (MICRO, ROWS, D), 1.0, 6.0, ((2, 32),)),
        "base_weight": normal_values(streams_of[2], (LAYERS, D, D), D ** -0.5, 0.0625, ((0, 4), (2, 32))),
        "norm_gain": draw_norm_gain(jax.random.fold_in(streams_of[8], 71), 0),
        "adapter_a": normal_values(streams_of[4], (LAYERS, ADAPTERS, RANK, D), D ** -0.5, 0.0625, ((0, 4), (3, 32))),
        "adapter_b": normal_values(streams_of[5], (LAYERS, ADAPTERS, RANK, D), RANK ** -0.5, 1.0, ((0, 4), (3, 32))),
        "seg_ids": jax.vmap(lambda own: jnp.searchsorted(jnp.cumsum(uneven_parts(own, ADAPTERS, ROWS, MOST, 2)), jnp.arange(ROWS), side="right"))(jax.random.split(streams_of[6], MICRO)).reshape((MICRO, ROWS)).astype(jnp.int32),
        "live_counts": touch_ends(jax.random.randint(streams_of[7], (MICRO, ADAPTERS), 1, MOST + 1), jax.random.fold_in(streams_of[7], 1), 1, MOST).astype(jnp.int32),
    }


EPSILON = 1e-06
SCALING = 2.0

def segment_tables(segment_row, live_row, adapter_count):
    row_count = segment_row.shape[0]
    labels = jnp.arange(adapter_count, dtype=jnp.int32)
    member = (segment_row[:, None] == labels[None, :]).astype(jnp.int32)
    counts = lax.optimization_barrier(jnp.sum(member, axis=0))
    before = (labels[:, None] < labels[None, :]).astype(jnp.int32)
    starts = lax.optimization_barrier(jnp.sum(counts[:, None] * before, axis=0))
    row_start = lax.optimization_barrier(jnp.sum(member * starts[None, :], axis=1))
    row_limit = lax.optimization_barrier(jnp.sum(member * jnp.minimum(live_row, counts)[None, :], axis=1))
    position = jnp.arange(row_count, dtype=jnp.int32) - row_start
    return (member.astype(jnp.float32), position < row_limit)

def spread_rank(values, member):
    joined = member[:, :, None] * values.astype(jnp.float32)[:, None, :]
    return joined.reshape(values.shape[0], -1).astype(jnp.bfloat16)

def select_rank(parts, member, rank):
    shaped = parts.reshape(parts.shape[0], member.shape[1], rank)
    return jnp.einsum('ra,rak->rk', member, shaped)

def frozen_grad(grad_out, weight, blocks):
    row_count = grad_out.shape[0]
    width = weight.shape[0]
    block = width // blocks
    pieces_grad = grad_out.reshape(row_count, blocks, block).transpose(1, 0, 2)
    pieces_weight = weight.reshape(width, blocks, block).transpose(1, 0, 2)

    def step(total, pair):
        term = lax.dot_general(pair[0], pair[1], (((1,), (1,)), ((), ())), preferred_element_type=jnp.float32)
        rounded = lax.optimization_barrier(term.astype(jnp.bfloat16))
        return (total + rounded.astype(jnp.float32), None)
    start_total = jnp.zeros((row_count, width), jnp.float32)
    total, unused = lax.scan(step, start_total, (pieces_grad, pieces_weight))
    return total

def reference(tokens_in, cotangent, base_weight, norm_gain, adapter_a, adapter_b, seg_ids, live_counts):
    layer_count = base_weight.shape[0]
    micro_count = tokens_in.shape[0]
    adapter_count = adapter_a.shape[1]
    rank = adapter_a.shape[2]
    width = base_weight.shape[1]
    tables = [segment_tables(seg_ids[slot], live_counts[slot], adapter_count) for slot in range(micro_count)]
    current = [tokens_in[slot] for slot in range(micro_count)]
    records = []
    layer_outputs = []
    for layer in range(layer_count):
        gain_f = norm_gain[layer].astype(jnp.float32)
        down_flat = adapter_a[layer].reshape(adapter_count * rank, width)
        up_flat = adapter_b[layer].reshape(adapter_count * rank, width)
        layer_records = []
        results = []
        for slot in range(micro_count):
            member = tables[slot][0]
            inputs = current[slot]
            values = inputs.astype(jnp.float32)
            inverse = lax.rsqrt(lax.optimization_barrier(jnp.mean(values * values, axis=1)) + EPSILON)
            normed = (values * inverse[:, None] * gain_f[None, :]).astype(jnp.bfloat16)
            down_parts = lax.dot_general(normed, down_flat, (((1,), (1,)), ((), ())), preferred_element_type=jnp.float32)
            down_proj = select_rank(down_parts, member, rank).astype(jnp.bfloat16)
            adapter_out = jnp.dot(spread_rank(down_proj, member), up_flat, preferred_element_type=jnp.float32)
            frozen_out = jnp.dot(normed, base_weight[layer], preferred_element_type=jnp.float32)
            result = (values + frozen_out + SCALING * adapter_out).astype(jnp.bfloat16)
            layer_records.append((inputs, normed, down_proj, inverse))
            results.append(result)
        records.append(layer_records)
        layer_outputs.append(jnp.stack(results))
        current = results
    grads_out = []
    for slot in range(micro_count):
        live_rows = tables[slot][1]
        grads_out.append(jnp.where(live_rows[:, None], cotangent[slot], jnp.zeros_like(cotangent[slot])))
    grad_a_layers = [None] * layer_count
    grad_b_layers = [None] * layer_count
    for layer in range(layer_count - 1, -1, -1):
        gain_f = norm_gain[layer].astype(jnp.float32)
        down_flat = adapter_a[layer].reshape(adapter_count * rank, width)
        up_flat = adapter_b[layer].reshape(adapter_count * rank, width)
        total_down = jnp.zeros((adapter_count * rank, width), jnp.float32)
        total_up = jnp.zeros((adapter_count * rank, width), jnp.float32)
        next_grads = []
        for slot in range(micro_count):
            member = tables[slot][0]
            inputs, normed, down_proj, inverse = records[layer][slot]
            grad_out = grads_out[slot]
            spread_down = spread_rank(down_proj, member)
            total_up = total_up + SCALING * lax.dot_general(spread_down, grad_out, (((0,), (0,)), ((), ())), preferred_element_type=jnp.float32)
            up_parts = lax.dot_general(grad_out, up_flat, (((1,), (1,)), ((), ())), preferred_element_type=jnp.float32)
            grad_down_proj = (SCALING * select_rank(up_parts, member, rank)).astype(jnp.bfloat16)
            spread_grad = spread_rank(grad_down_proj, member)
            total_down = total_down + lax.dot_general(spread_grad, normed, (((0,), (0,)), ((), ())), preferred_element_type=jnp.float32)
            adapter_part = jnp.dot(spread_grad, down_flat, preferred_element_type=jnp.float32)
            grad_normed = frozen_grad(grad_out, base_weight[layer], N_DP) + adapter_part
            values = inputs.astype(jnp.float32)
            norm_stat = lax.optimization_barrier(jnp.mean(values * gain_f[None, :] * grad_normed, axis=1))
            cubed = inverse * inverse * inverse
            grad_in = grad_out.astype(jnp.float32) + inverse[:, None] * gain_f[None, :] * grad_normed - values * cubed[:, None] * norm_stat[:, None]
            next_grads.append(grad_in.astype(jnp.bfloat16))
        grad_a_layers[layer] = total_down.reshape(adapter_count, rank, width)
        grad_b_layers[layer] = total_up.reshape(adapter_count, rank, width)
        grads_out = next_grads
    return (jnp.stack(layer_outputs), jnp.stack(grad_a_layers), jnp.stack(grad_b_layers))
```

```python
import jax
import jax.numpy as jnp
from jax import lax
from jax.sharding import PartitionSpec as P

EPSILON = 1e-06
SCALING = 2.0
XS, YS, CS = 4, 4, 2
BF = jnp.bfloat16
F32 = jnp.float32


def place(x, y, c):
    return (x * YS + y) * CS + c


ALONG_X = [[place(x, y, c) for x in range(XS)] for y in range(YS) for c in range(CS)]
ALONG_Y = [[place(x, y, c) for y in range(YS)] for x in range(XS) for c in range(CS)]
ALONG_XY = [[place(x, y, c) for x in range(XS) for y in range(YS)] for c in range(CS)]
SIBLING = [(i, i ^ 1) for i in range(XS * YS * CS)]


def exchange(chunks, groups):
    return lax.all_to_all(chunks, "dp", 0, 0, axis_index_groups=groups)


def spread_out(block, groups):
    return exchange(jnp.broadcast_to(block[None], (4,) + block.shape), groups)


def swap_cores(block):
    return lax.ppermute(block, "dp", SIBLING)


def split_pair(row):
    high = row.astype(BF)
    low = (row - high.astype(F32)).astype(BF)
    return high, low


def pack(main, ranks, row):
    high, low = split_pair(row)
    filler = jnp.zeros((14, row.shape[-1]), BF)
    return jnp.concatenate([main.astype(BF), ranks.astype(BF), high, low, filler], axis=0)


def extras(chunks, width):
    rest = chunks[..., width:, :].astype(F32)
    rank = rest.shape[-2] - 16
    return rest[..., :rank, :], rest[..., rank : rank + 1, :] + rest[..., rank + 1 : rank + 2, :]


def tables_of(seg_ids, live_counts, adapters):
    micro, rows = seg_ids.shape
    labels = jnp.arange(adapters, dtype=jnp.int32)
    member = (seg_ids[:, None, :] == labels[None, :, None]).astype(jnp.int32)
    counts = jnp.sum(member, axis=2)
    before = (labels[:, None] < labels[None, :]).astype(jnp.int32)
    starts = jnp.sum(counts[:, :, None] * before[None], axis=1)
    row_start = jnp.sum(member * starts[:, :, None], axis=1)
    row_limit = jnp.sum(member * jnp.minimum(live_counts, counts)[:, :, None], axis=1)
    live = jnp.arange(rows, dtype=jnp.int32)[None] - row_start < row_limit
    whole = member.astype(F32).transpose(1, 0, 2).reshape(adapters, micro * rows)
    return whole, live.reshape(micro * rows)


def select_rank(parts, member):
    shaped = parts.reshape(member.shape[0], -1, parts.shape[-1])
    return jnp.sum(shaped * member[:, None, :], axis=0)


def spread_rank(values, member):
    joined = member[:, None, :] * values.astype(F32)[None]
    return joined.reshape(-1, values.shape[-1]).astype(BF)


def dot(left, right, dims):
    return lax.dot_general(left, right, (dims, ((), ())), preferred_element_type=F32)


def on_device(
    tokens_in, cotangent, base_weight, norm_gain, adapter_a, adapter_b, seg_ids, live_counts
):
    section = lax.axis_index("section")
    core = lax.axis_index("dp") % CS
    micro, rows, cols = tokens_in.shape
    total = micro * rows
    adapters, rank = adapter_a.shape[1:3]
    width = base_weight.shape[1]
    gain = norm_gain[0].astype(F32)[:, None]
    a_flat = adapter_a[0].reshape(adapters * rank, cols)
    b_flat = adapter_b[0].reshape(adapters * rank, cols)
    member, live = tables_of(seg_ids, live_counts, adapters)
    block = exchange(base_weight[0].reshape(XS, width // XS, cols), ALONG_X)
    block = block.reshape(XS, YS, CS, cols, cols)
    own_rows = lax.dynamic_index_in_dim(block, core, 2, keepdims=False)
    sib_rows = lax.dynamic_index_in_dim(block, 1 - core, 2, keepdims=False)
    tokens = tokens_in.reshape(total, cols).T
    target = jnp.where(live[None, :], cotangent.reshape(total, cols).T, jnp.zeros((), BF))

    def forward(current):
        values = current.astype(F32)
        scaled = (values * gain).astype(BF)
        ranks = select_rank(dot(a_flat, scaled, ((1,), (0,))), member)
        squares = jnp.sum(values * values, axis=0, keepdims=True)
        got = spread_out(pack(scaled, ranks, squares), ALONG_Y)
        other = swap_cores(got)
        partial = dot(own_rows, got[:, :cols], ((1, 2), (0, 1))) + dot(
            sib_rows, other[:, :cols], ((1, 2), (0, 1))
        )
        ranks, squares = extras(got, cols)
        ranks_o, squares_o = extras(other, cols)
        ranks = jnp.sum(ranks + ranks_o, axis=0)
        squares = jnp.sum(squares + squares_o, axis=0)
        send = jnp.stack([pack(partial[i], ranks, squares) for i in range(XS)])
        got = exchange(send, ALONG_X)
        frozen = jnp.sum(got[:, :cols].astype(F32), axis=0)
        ranks, squares = extras(got, cols)
        ranks = jnp.sum(ranks, axis=0)
        inverse = lax.rsqrt(jnp.sum(squares, axis=0) / width + EPSILON)
        down = (ranks * inverse).astype(BF)
        adapter = dot(b_flat, spread_rank(down, member), ((0,), (0,)))
        result = (values + frozen * inverse + SCALING * adapter).astype(BF)
        return result, frozen, ranks, inverse, down

    def backward(grad, values, frozen, down_raw, inverse):
        ranks = select_rank(dot(b_flat, grad, ((1,), (0,))), member)
        stat = jnp.sum(grad.astype(F32) * frozen, axis=0, keepdims=True)
        got = spread_out(pack(grad, ranks, stat), ALONG_X)
        mains = got[:, :cols]
        own = dot(own_rows, mains, ((0, 3), (0, 1)))
        sib = dot(sib_rows, mains, ((0, 3), (0, 1)))
        ranks, stat = extras(got, cols)
        ranks, stat = jnp.sum(ranks, axis=0), jnp.sum(stat, axis=0)
        other = swap_cores(jnp.stack([pack(sib[i], ranks, stat) for i in range(YS)]))
        ranks_o, stat_o = extras(other[0], cols)
        ranks, stat = ranks + ranks_o, stat + stat_o
        both = own + other[:, :cols].astype(F32)
        got = exchange(jnp.stack([pack(both[i], ranks, stat) for i in range(YS)]), ALONG_Y)
        frozen_back = jnp.sum(got[:, :cols].astype(F32), axis=0)
        ranks, stat = extras(got, cols)
        grad_down = (SCALING * jnp.sum(ranks, axis=0)).astype(BF)
        stat = jnp.sum(stat, axis=0) + jnp.sum(
            grad_down.astype(F32) * down_raw, axis=0, keepdims=True
        )
        adapter = dot(a_flat, spread_rank(grad_down, member), ((0,), (0,)))
        normed_grad = frozen_back + adapter
        cubed = inverse * inverse * inverse
        grad_in = (
            grad.astype(F32) + inverse * gain * normed_grad - values * cubed * (stat / width)
        )
        return grad_in.astype(BF)

    current = jnp.where(section == 0, tokens, jnp.zeros_like(tokens))
    for moment in range(4):
        result, frozen, down_raw, inverse, down = forward(current)
        if moment < 3:
            received = lax.ppermute(result, "section", [(i, i + 1) for i in range(3)])
            current = jnp.where(section == moment + 1, received, current)
    values = current.astype(F32)
    grad = jnp.where(section == 3, target, jnp.zeros_like(target))
    for moment in range(3):
        grad_in = backward(grad, values, frozen, down_raw, inverse)
        received = lax.ppermute(grad_in, "section", [(i + 1, i) for i in range(3)])
        grad = jnp.where(section == 2 - moment, received, grad)
    ranks = select_rank(dot(b_flat, grad, ((1,), (0,))), member)
    ranks = ranks + lax.ppermute(ranks, "dp", SIBLING)
    ranks = ranks.astype(BF)
    ranks = exchange(jnp.broadcast_to(ranks[None], (XS * YS,) + ranks.shape), ALONG_XY)
    grad_down = (SCALING * jnp.sum(ranks.astype(F32), axis=0)).astype(BF)
    normed = (values * inverse * gain).astype(BF)
    grad_a = dot(spread_rank(grad_down, member), normed, ((1,), (1,)))
    grad_b = SCALING * dot(spread_rank(down, member), grad, ((1,), (1,)))
    section_out = result.T.reshape(1, micro, rows, cols)
    shape = (1, adapters, rank, cols)
    return section_out, grad_a.reshape(shape), grad_b.reshape(shape)


def solution(mesh):
    in_specs = (
        P(None, None, "dp"),
        P(None, None, "dp"),
        P("section", None, "dp"),
        P("section", "dp"),
        P("section", None, None, "dp"),
        P("section", None, None, "dp"),
        P(),
        P(),
    )
    out_specs = (
        P("section", None, None, "dp"),
        P("section", None, None, "dp"),
        P("section", None, None, "dp"),
    )
    return jax.shard_map(
        on_device, mesh=mesh, in_specs=in_specs, out_specs=out_specs, check_vma=False
    )
```

```python
import functools

import jax
import jax.numpy as jnp
from jax import lax
from jax.experimental import pallas as pl
from jax.experimental.pallas import tpu as pltpu
from jax.sharding import PartitionSpec as P

EPSILON = 1e-06
SCALING = 2.0
XS, YS, CS = 4, 4, 2
BF = jnp.bfloat16
F32 = jnp.float32
VM = pl.BlockSpec(memory_space=pltpu.VMEM)
SM = pl.BlockSpec(memory_space=pltpu.SMEM)
PARAMS = pltpu.CompilerParams(vmem_limit_bytes=48 << 20)


def place(x, y, c):
    return (x * YS + y) * CS + c


ALONG_X = [[place(x, y, c) for x in range(XS)] for y in range(YS) for c in range(CS)]
ALONG_Y = [[place(x, y, c) for y in range(YS)] for x in range(XS) for c in range(CS)]
ALONG_XY = [[place(x, y, c) for x in range(XS) for y in range(YS)] for c in range(CS)]
SIBLING = [(i, i ^ 1) for i in range(XS * YS * CS)]


def exchange(chunks, groups):
    return lax.all_to_all(chunks, "dp", 0, 0, axis_index_groups=groups)


def swap_cores(block):
    return lax.ppermute(block, "dp", SIBLING)


def tables_of(seg_ids, live_counts, adapters):
    micro, rows = seg_ids.shape
    labels = jnp.arange(adapters, dtype=jnp.int32)
    member = (seg_ids[:, None, :] == labels[None, :, None]).astype(jnp.int32)
    counts = jnp.sum(member, axis=2)
    before = (labels[:, None] < labels[None, :]).astype(jnp.int32)
    starts = jnp.sum(counts[:, :, None] * before[None], axis=1)
    row_start = jnp.sum(member * starts[:, :, None], axis=1)
    row_limit = jnp.sum(member * jnp.minimum(live_counts, counts)[:, :, None], axis=1)
    live = jnp.arange(rows, dtype=jnp.int32)[None] - row_start < row_limit
    whole = member.astype(F32).transpose(1, 0, 2).reshape(adapters, micro * rows)
    return whole, live.reshape(micro * rows)


def dot(left, right, dims=((1,), (0,))):
    return lax.dot_general(left, right, (dims, ((), ())), preferred_element_type=F32)


def tail_of(ranks, row):
    high = row.astype(BF).astype(F32)
    low = row - high
    index = lax.broadcasted_iota(jnp.int32, (16, row.shape[1]), 0)
    tail = jnp.where(index == 0, high, jnp.where(index == 1, low, jnp.zeros_like(high)))
    return jnp.concatenate([ranks, tail], axis=0).astype(BF)


def extras(chunks, cols, rank):
    ranks, row = None, None
    for j in range(chunks.shape[0]):
        part = chunks[j, cols : cols + rank].astype(F32)
        tail = chunks[j, cols + rank :].astype(F32)
        one = tail[0:1] + tail[1:2]
        ranks = part if ranks is None else ranks + part
        row = one if row is None else row + one
    return ranks, row


def select_rank(parts, member_ref, rank):
    total = None
    for a in range(member_ref.shape[0]):
        part = parts[a * rank : (a + 1) * rank] * member_ref[a : a + 1, :]
        total = part if total is None else total + part
    return total


def spread_rank(values, member_ref, store):
    rank = values.shape[0]
    for a in range(member_ref.shape[0]):
        store[a * rank : (a + 1) * rank] = (values * member_ref[a : a + 1, :]).astype(BF)


def pre_forward(flag, received, older, gain, a_flat, member, current, sent):
    cols, rank = received.shape[0], a_flat.shape[0] // member.shape[0]
    fresh = jnp.where(flag[0] > 0, received[...].astype(F32), older[...].astype(F32))
    current[...] = fresh.astype(BF)
    scaled = (fresh * gain[...]).astype(BF)
    ranks = select_rank(dot(a_flat[...], scaled), member, rank)
    tail = tail_of(ranks, jnp.sum(fresh * fresh, axis=0, keepdims=True))
    for j in range(sent.shape[0]):
        sent[j, :cols] = scaled
        sent[j, cols:] = tail


def mid_forward(core, got, other, weight, sent, joined):
    cols, rank = weight.shape[1], got.shape[1] - weight.shape[1] - 16

    @pl.when(pl.program_id(0) == 0)
    def _():
        for y in range(YS):
            mine = pl.multiple_of((y * CS + core[0]) * cols, cols)
            theirs = pl.multiple_of((y * CS + 1 - core[0]) * cols, cols)
            joined[pl.ds(mine, cols)] = got[y, :cols]
            joined[pl.ds(theirs, cols)] = other[y, :cols]

    sent[0, :cols] = dot(weight[0], joined[...]).astype(BF)
    ranks, row = extras(got, cols, rank)
    ranks_o, row_o = extras(other, cols, rank)
    sent[0, cols:] = tail_of(ranks + ranks_o, row + row_o)


def post_forward(
    width, got, current, b_turned, member, result, frozen, down_raw, inverse, down, store
):
    cols, rank = current.shape[0], down.shape[0]
    total = got[0, :cols].astype(F32)
    for j in range(1, XS):
        total = total + got[j, :cols].astype(F32)
    ranks, row = extras(got, cols, rank)
    scale = lax.rsqrt(row / width + EPSILON)
    kept = (ranks * scale).astype(BF)
    spread_rank(kept.astype(F32), member, store)
    adapter = dot(b_turned[...], store[...])
    result[...] = (current[...].astype(F32) + total * scale + SCALING * adapter).astype(BF)
    frozen[...] = total
    down_raw[...] = ranks
    inverse[...] = scale
    down[...] = kept


def pre_backward(flag, received, older, frozen, b_flat, member, grad, sent):
    cols, rank = received.shape[0], b_flat.shape[0] // member.shape[0]
    fresh = jnp.where(flag[0] > 0, received[...].astype(F32), older[...].astype(F32))
    kept = fresh.astype(BF)
    grad[...] = kept
    ranks = select_rank(dot(b_flat[...], kept), member, rank)
    tail = tail_of(ranks, jnp.sum(fresh * frozen[...], axis=0, keepdims=True))
    for j in range(sent.shape[0]):
        sent[j, :cols] = kept
        sent[j, cols:] = tail


def mid_backward(core, got, weight, *rest):
    sent = rest[-1]
    cols, rank = weight.shape[-1], got.shape[1] - weight.shape[-1] - 16
    total = dot(weight[0, 0, 0], got[0, :cols])
    for j in range(1, XS):
        total = total + dot(weight[j, 0, 0], got[j, :cols])
    ranks, row = extras(got, cols, rank)
    if len(rest) > 1:
        other = rest[0]
        total = total + other[0, :cols].astype(F32)
        ranks_o, row_o = extras(other, cols, rank)
        ranks, row = ranks + ranks_o, row + row_o
    sent[0, :cols] = total.astype(BF)
    sent[0, cols:] = tail_of(ranks, row)


def post_backward(
    width, got, grad, current, a_turned, member, down_raw, inverse, gain, grad_in, store
):
    cols, rank = current.shape[0], down_raw.shape[0]
    total = got[0, :cols].astype(F32)
    for j in range(1, YS):
        total = total + got[j, :cols].astype(F32)
    ranks, row = extras(got, cols, rank)
    grad_down = (SCALING * ranks).astype(BF).astype(F32)
    spread_rank(grad_down, member, store)
    normed_grad = total + dot(a_turned[...], store[...])
    stat = (row + jnp.sum(grad_down * down_raw[...], axis=0, keepdims=True)) / width
    scale = inverse[...]
    grad_in[...] = (
        grad[...].astype(F32)
        + scale * gain[...] * normed_grad
        - current[...].astype(F32) * (scale * scale * scale * stat)
    ).astype(BF)


def outer_up(down, grad, member, grad_b, store):
    spread_rank(SCALING * down[...].astype(F32), member, store)
    grad_b[...] = dot(store[...], grad[...], ((1,), (1,)))


def outer_down(got, current, inverse, gain, member, grad_a, store):
    ranks = got[0].astype(F32)
    for j in range(1, got.shape[0]):
        ranks = ranks + got[j].astype(F32)
    grad_down = (SCALING * ranks).astype(BF).astype(F32)
    spread_rank(grad_down, member, store)
    normed = (current[...].astype(F32) * inverse[...] * gain[...]).astype(BF)
    grad_a[...] = dot(store[...], normed, ((1,), (1,)))


def whole_call(body, name, outs, ins, scratch=(), scalars=0):
    return pl.pallas_call(
        body,
        out_shape=[jax.ShapeDtypeStruct(s, d) for s, d in outs],
        in_specs=[SM] * scalars + [VM] * (len(ins) - scalars),
        out_specs=[VM] * len(outs),
        scratch_shapes=list(scratch),
        compiler_params=PARAMS,
        name=name,
    )(*ins)


def on_device(
    tokens_in, cotangent, base_weight, norm_gain, adapter_a, adapter_b, seg_ids, live_counts
):
    section = lax.axis_index("section")
    core = (lax.axis_index("dp") % CS).astype(jnp.int32).reshape(1)
    micro, rows, cols = tokens_in.shape
    total = micro * rows
    adapters, rank = adapter_a.shape[1:3]
    width = base_weight.shape[1]
    tall = cols + rank + 16
    gain = norm_gain[0].astype(F32)[:, None]
    a_flat = adapter_a[0].reshape(adapters * rank, cols)
    b_flat = adapter_b[0].reshape(adapters * rank, cols)
    a_turned, b_turned = a_flat.T, b_flat.T
    member, live = tables_of(seg_ids, live_counts, adapters)
    block = exchange(base_weight[0].reshape(XS, width // XS, cols), ALONG_X)
    turned = block.transpose(0, 2, 1)
    block = block.reshape(XS, YS, CS, cols, cols)
    tokens = tokens_in.reshape(total, cols).T
    target = jnp.where(live[None, :], cotangent.reshape(total, cols).T, jnp.zeros((), BF))
    store = pltpu.VMEM((adapters * rank, total), BF)
    payload = ((XS, tall, total), BF)
    main = ((cols, total), BF)

    def flag_of(at):
        return (section == at).astype(jnp.int32).reshape(1)

    def mid_call(name, got, other=None):
        chosen = (lambda c: c[0]) if other is not None else (lambda c: 1 - c[0])
        specs = [
            pl.BlockSpec((XS, tall, total), lambda i, c: (0, 0, 0)),
            pl.BlockSpec((XS, 1, 1, cols, cols), lambda i, c: (0, i, chosen(c), 0, 0)),
        ]
        ins = [got, block]
        if other is not None:
            specs.append(pl.BlockSpec((1, tall, total), lambda i, c: (i, 0, 0)))
            ins.append(other)
        return pl.pallas_call(
            mid_backward,
            grid_spec=pltpu.PrefetchScalarGridSpec(
                num_scalar_prefetch=1,
                grid=(YS,),
                in_specs=specs,
                out_specs=pl.BlockSpec((1, tall, total), lambda i, c: (i, 0, 0)),
            ),
            out_shape=jax.ShapeDtypeStruct(*payload),
            compiler_params=PARAMS,
            name=name,
        )(core, *ins)

    def forward(flag, received, older):
        current, sent = whole_call(
            pre_forward,
            "pre_forward",
            [main, payload],
            [flag, received, older, gain, a_flat, member],
            scalars=1,
        )
        got = exchange(sent, ALONG_Y)
        other = swap_cores(got)
        sent = pl.pallas_call(
            mid_forward,
            grid_spec=pltpu.PrefetchScalarGridSpec(
                num_scalar_prefetch=1,
                grid=(XS,),
                in_specs=[
                    pl.BlockSpec((YS, tall, total), lambda i, c: (0, 0, 0)),
                    pl.BlockSpec((YS, tall, total), lambda i, c: (0, 0, 0)),
                    pl.BlockSpec((1, cols, width // XS), lambda i, c: (i, 0, 0)),
                ],
                out_specs=pl.BlockSpec((1, tall, total), lambda i, c: (i, 0, 0)),
                scratch_shapes=[pltpu.VMEM((width // XS, total), BF)],
            ),
            out_shape=jax.ShapeDtypeStruct(*payload),
            compiler_params=PARAMS,
            name="mid_forward",
        )(core, got, other, turned)
        got = exchange(sent, ALONG_X)
        outs = whole_call(
            functools.partial(post_forward, width),
            "post_forward",
            [
                main,
                ((cols, total), F32),
                ((rank, total), F32),
                ((1, total), F32),
                ((rank, total), BF),
            ],
            [got, current, b_turned, member],
            scratch=[store],
        )
        return current, outs

    def backward(flag, received, older, frozen, current, down_raw, inverse):
        grad, sent = whole_call(
            pre_backward,
            "pre_backward",
            [main, payload],
            [flag, received, older, frozen, b_flat, member],
            scalars=1,
        )
        got = exchange(sent, ALONG_X)
        other = swap_cores(mid_call("mid_backward_other", got))
        got = exchange(mid_call("mid_backward_own", got, other), ALONG_Y)
        (grad_in,) = whole_call(
            functools.partial(post_backward, width),
            "post_backward",
            [main],
            [got, grad, current, a_turned, member, down_raw, inverse, gain],
            scratch=[store],
        )
        return grad, grad_in

    received, current = tokens, jnp.zeros_like(tokens)
    for moment in range(4):
        current, outs = forward(flag_of(moment), received, current)
        if moment < 3:
            received = lax.ppermute(outs[0], "section", [(i, i + 1) for i in range(3)])
    result, frozen, down_raw, inverse, down = outs
    received, grad = target, jnp.zeros_like(target)
    for moment in range(3):
        grad, grad_in = backward(
            flag_of(3 - moment), received, grad, frozen, current, down_raw, inverse
        )
        received = lax.ppermute(grad_in, "section", [(i + 1, i) for i in range(3)])
    grad, sent = whole_call(
        pre_backward,
        "pre_last",
        [main, ((1, tall, total), BF)],
        [flag_of(0), received, grad, frozen, b_flat, member],
        scalars=1,
    )
    ranks = sent[0, cols : cols + rank].astype(F32)
    ranks = (ranks + lax.ppermute(ranks, "dp", SIBLING)).astype(BF)
    ranks = exchange(jnp.broadcast_to(ranks[None], (XS * YS,) + ranks.shape), ALONG_XY)
    (grad_b,) = whole_call(
        outer_up,
        "outer_up",
        [((adapters * rank, cols), F32)],
        [down, grad, member],
        scratch=[store],
    )
    (grad_a,) = whole_call(
        outer_down,
        "outer_down",
        [((adapters * rank, cols), F32)],
        [ranks, current, inverse, gain, member],
        scratch=[store],
    )
    section_out = result.T.reshape(1, micro, rows, cols)
    shape = (1, adapters, rank, cols)
    return section_out, grad_a.reshape(shape), grad_b.reshape(shape)


def solution(mesh):
    in_specs = (
        P(None, None, "dp"),
        P(None, None, "dp"),
        P("section", None, "dp"),
        P("section", "dp"),
        P("section", None, None, "dp"),
        P("section", None, None, "dp"),
        P(),
        P(),
    )
    out_specs = (
        P("section", None, None, "dp"),
        P("section", None, None, "dp"),
        P("section", None, None, "dp"),
    )
    return jax.shard_map(
        on_device, mesh=mesh, in_specs=in_specs, out_specs=out_specs, check_vma=False
    )
```

```python
import functools

import jax
import jax.numpy as jnp
from jax import lax
from jax.experimental import pallas as pl
from jax.experimental.pallas import tpu as pltpu
from jax.sharding import PartitionSpec as P

EPSILON = 1e-06
SCALING = 2.0
XS, YS, CS = 4, 4, 2
BF = jnp.bfloat16
F32 = jnp.float32
VM = pl.BlockSpec(memory_space=pltpu.VMEM)
SM = pl.BlockSpec(memory_space=pltpu.SMEM)
PARAMS = pltpu.CompilerParams(vmem_limit_bytes=48 << 20)


def place(x, y, c):
    return (x * YS + y) * CS + c


ALONG_X = [[place(x, y, c) for x in range(XS)] for y in range(YS) for c in range(CS)]
ALONG_Y = [[place(x, y, c) for y in range(YS)] for x in range(XS) for c in range(CS)]
ALONG_XY = [[place(x, y, c) for x in range(XS) for y in range(YS)] for c in range(CS)]
SIBLING = [(i, i ^ 1) for i in range(XS * YS * CS)]


def exchange(chunks, groups):
    return lax.all_to_all(chunks, "dp", 0, 0, axis_index_groups=groups)


def swap_cores(block):
    return lax.ppermute(block, "dp", SIBLING)


def tables_of(seg_ids, live_counts, adapters):
    micro, rows = seg_ids.shape
    labels = jnp.arange(adapters, dtype=jnp.int32)
    member = (seg_ids[:, None, :] == labels[None, :, None]).astype(jnp.int32)
    counts = jnp.sum(member, axis=2)
    before = (labels[:, None] < labels[None, :]).astype(jnp.int32)
    starts = jnp.sum(counts[:, :, None] * before[None], axis=1)
    row_start = jnp.sum(member * starts[:, :, None], axis=1)
    row_limit = jnp.sum(member * jnp.minimum(live_counts, counts)[:, :, None], axis=1)
    live = jnp.arange(rows, dtype=jnp.int32)[None] - row_start < row_limit
    whole = member.astype(F32).transpose(1, 0, 2).reshape(adapters, micro * rows)
    return whole, live.reshape(micro * rows)


def dot(left, right, dims=((1,), (0,))):
    return lax.dot_general(left, right, (dims, ((), ())), preferred_element_type=F32)


def tail_of(ranks, row):
    high = row.astype(BF).astype(F32)
    low = row - high
    index = lax.broadcasted_iota(jnp.int32, (16, row.shape[1]), 0)
    tail = jnp.where(index == 0, high, jnp.where(index == 1, low, jnp.zeros_like(high)))
    return jnp.concatenate([ranks, tail], axis=0).astype(BF)


def extras(chunks, cols, rank):
    ranks, row = None, None
    for j in range(chunks.shape[0]):
        part = chunks[j, cols : cols + rank].astype(F32)
        tail = chunks[j, cols + rank :].astype(F32)
        one = tail[0:1] + tail[1:2]
        ranks = part if ranks is None else ranks + part
        row = one if row is None else row + one
    return ranks, row


def select_rank(parts, member_ref, rank):
    total = None
    for a in range(member_ref.shape[0]):
        part = parts[a * rank : (a + 1) * rank] * member_ref[a : a + 1, :]
        total = part if total is None else total + part
    return total


def spread_rank(values, member_ref, store):
    rank = values.shape[0]
    for a in range(member_ref.shape[0]):
        store[a * rank : (a + 1) * rank] = (values * member_ref[a : a + 1, :]).astype(BF)


def fill(flags, sent, main, tail, alt):
    cols = main.shape[0]

    def write():
        for j in range(sent.shape[0]):
            sent[j, :cols] = main
            sent[j, cols:] = tail

    if alt is None:
        write()
        return
    pl.when(flags[1] == 0)(write)

    @pl.when(flags[1] > 0)
    def _():
        sent[...] = alt[...]


def pre_forward(flags, received, older, gain, a_flat, member, *rest):
    alt, current, sent = rest if len(rest) == 3 else (None,) + rest
    rank = a_flat.shape[0] // member.shape[0]
    fresh = jnp.where(flags[0] > 0, received[...].astype(F32), older[...].astype(F32))
    current[...] = fresh.astype(BF)
    scaled = (fresh * gain[...]).astype(BF)
    ranks = select_rank(dot(a_flat[...], scaled), member, rank)
    tail = tail_of(ranks, jnp.sum(fresh * fresh, axis=0, keepdims=True))
    fill(flags, sent, scaled, tail, alt)


def mid_forward(info, got, other, weight, *rest):
    alt, sent, joined = rest if len(rest) == 3 else (None,) + rest
    cols, rank = weight.shape[1], got.shape[1] - weight.shape[1] - 16
    core = info[0]

    @pl.when(pl.program_id(0) == 0)
    def _():
        for y in range(YS):
            mine = pl.multiple_of((y * CS + core) * cols, cols)
            theirs = pl.multiple_of((y * CS + 1 - core) * cols, cols)
            joined[pl.ds(mine, cols)] = got[y, :cols]
            joined[pl.ds(theirs, cols)] = other[y, :cols]

    def write():
        sent[0, :cols] = dot(weight[0], joined[...]).astype(BF)
        ranks, row = extras(got, cols, rank)
        ranks_o, row_o = extras(other, cols, rank)
        sent[0, cols:] = tail_of(ranks + ranks_o, row + row_o)

    if alt is None:
        write()
        return
    pl.when(info[1] == 0)(write)

    @pl.when(info[1] > 0)
    def _():
        sent[...] = alt[...]


def post_forward(
    width, got, current, b_turned, member, result, frozen, down_raw, inverse, down, store
):
    cols, rank = current.shape[0], down.shape[0]
    total = got[0, :cols].astype(F32)
    for j in range(1, XS):
        total = total + got[j, :cols].astype(F32)
    ranks, row = extras(got, cols, rank)
    scale = lax.rsqrt(row / width + EPSILON)
    kept = (ranks * scale).astype(BF)
    spread_rank(kept.astype(F32), member, store)
    adapter = dot(b_turned[...], store[...])
    result[...] = (current[...].astype(F32) + total * scale + SCALING * adapter).astype(BF)
    frozen[...] = total
    down_raw[...] = ranks
    inverse[...] = scale
    down[...] = kept


def post_forward_turn(
    width, got, current, b_turned, member, ahead, result, frozen, down_raw, inverse, down, small, store
):
    post_forward(
        width, got, current, b_turned, member, result, frozen, down_raw, inverse, down, store
    )
    values = result[...].astype(F32)
    squares = jnp.sum(values * values, axis=0, keepdims=True)
    stat = jnp.sum(values * ahead[...], axis=0, keepdims=True)
    index = lax.broadcasted_iota(jnp.int32, (16, values.shape[1]), 0)
    tail = jnp.zeros((16, values.shape[1]), F32)
    for at, row in ((0, squares), (2, stat)):
        high = row.astype(BF).astype(F32)
        tail = jnp.where(index == at, high, jnp.where(index == at + 1, row - high, tail))
    tail = tail.astype(BF)
    for j in range(small.shape[0]):
        small[j] = tail


def turn(width, flags, small, result, target, ahead, frozen, b_flat, member, grad, sent):
    rank = b_flat.shape[0] // member.shape[0]
    rows = jnp.sum(small[...].astype(F32), axis=0)
    scale = lax.rsqrt((rows[0:1] + rows[1:2]) / width + EPSILON)
    stat = (rows[2:3] + rows[3:4]) / width
    first = target[...].astype(F32)
    fresh = (
        first + scale * ahead[...] - result[...].astype(F32) * (scale * scale * scale * stat)
    )
    kept = jnp.where(flags[0] > 0, fresh, first).astype(BF)
    grad[...] = kept
    ranks = select_rank(dot(b_flat[...], kept), member, rank)
    row = jnp.sum(kept.astype(F32) * frozen[...], axis=0, keepdims=True)
    fill(flags, sent, kept, tail_of(ranks, row), None)


def pre_backward(flags, received, older, frozen, b_flat, member, *rest):
    alt, grad, sent = rest if len(rest) == 3 else (None,) + rest
    rank = b_flat.shape[0] // member.shape[0]
    fresh = jnp.where(flags[0] > 0, received[...].astype(F32), older[...].astype(F32))
    kept = fresh.astype(BF)
    grad[...] = kept
    ranks = select_rank(dot(b_flat[...], kept), member, rank)
    tail = tail_of(ranks, jnp.sum(fresh * frozen[...], axis=0, keepdims=True))
    fill(flags, sent, kept, tail, alt)


def pre_target(target, b_flat, member, sent):
    rank = b_flat.shape[0] // member.shape[0]
    kept = target[...]
    ranks = select_rank(dot(b_flat[...], kept), member, rank)
    tail = tail_of(ranks, jnp.zeros((1, kept.shape[1]), F32))
    fill(None, sent, kept, tail, None)


def mid_backward_other(info, got, weight, sent):
    cols, rank = weight.shape[-1], got.shape[1] - weight.shape[-1] - 16
    total = dot(weight[0, 0, 0], got[0, :cols])
    for j in range(1, XS):
        total = total + dot(weight[j, 0, 0], got[j, :cols])
    sent[0, :cols] = total.astype(BF)
    sent[0, cols:] = tail_of(*extras(got, cols, rank))


def mid_backward_own(info, got, weight, other, *rest):
    alt, sent = rest if len(rest) == 2 else (None,) + rest
    cols, rank = weight.shape[-1], got.shape[1] - weight.shape[-1] - 16

    def write():
        total = other[0, :cols].astype(F32)
        for j in range(XS):
            total = total + dot(weight[j, 0, 0], got[j, :cols])
        sent[0, :cols] = total.astype(BF)
        ranks, row = extras(got, cols, rank)
        ranks_o, row_o = extras(other, cols, rank)
        sent[0, cols:] = tail_of(ranks + ranks_o, row + row_o)

    if alt is None:
        write()
        return
    pl.when(info[1] == 0)(write)

    @pl.when(info[1] > 0)
    def _():
        sent[...] = alt[...]


def collect(got, a_turned, member, rank, store):
    cols = a_turned.shape[0]
    total = got[0, :cols].astype(F32)
    for j in range(1, YS):
        total = total + got[j, :cols].astype(F32)
    ranks, row = extras(got, cols, rank)
    grad_down = (SCALING * ranks).astype(BF).astype(F32)
    spread_rank(grad_down, member, store)
    return total + dot(a_turned[...], store[...]), grad_down, row


def post_target(rank, got, a_turned, member, gain, ahead, store):
    normed_grad, _, _ = collect(got, a_turned, member, rank, store)
    ahead[...] = gain[...] * normed_grad


def post_backward(
    width, got, grad, current, a_turned, member, down_raw, inverse, gain, grad_in, store
):
    normed_grad, grad_down, row = collect(got, a_turned, member, down_raw.shape[0], store)
    stat = (row + jnp.sum(grad_down * down_raw[...], axis=0, keepdims=True)) / width
    scale = inverse[...]
    grad_in[...] = (
        grad[...].astype(F32)
        + scale * gain[...] * normed_grad
        - current[...].astype(F32) * (scale * scale * scale * stat)
    ).astype(BF)


def outer_up(down, grad, member, grad_b, store):
    spread_rank(SCALING * down[...].astype(F32), member, store)
    grad_b[...] = dot(store[...], grad[...], ((1,), (1,)))


def outer_down(got, current, inverse, gain, member, grad_a, store):
    ranks = got[0].astype(F32)
    for j in range(1, got.shape[0]):
        ranks = ranks + got[j].astype(F32)
    grad_down = (SCALING * ranks).astype(BF).astype(F32)
    spread_rank(grad_down, member, store)
    normed = (current[...].astype(F32) * inverse[...] * gain[...]).astype(BF)
    grad_a[...] = dot(store[...], normed, ((1,), (1,)))


def whole_call(body, name, outs, ins, scratch=(), scalars=0):
    return pl.pallas_call(
        body,
        out_shape=[jax.ShapeDtypeStruct(s, d) for s, d in outs],
        in_specs=[SM] * scalars + [VM] * (len(ins) - scalars),
        out_specs=[VM] * len(outs),
        scratch_shapes=list(scratch),
        compiler_params=PARAMS,
        name=name,
    )(*ins)


def on_device(
    tokens_in, cotangent, base_weight, norm_gain, adapter_a, adapter_b, seg_ids, live_counts
):
    section = lax.axis_index("section")
    core = (lax.axis_index("dp") % CS).astype(jnp.int32)
    micro, rows, cols = tokens_in.shape
    total = micro * rows
    adapters, rank = adapter_a.shape[1:3]
    width = base_weight.shape[1]
    tall = cols + rank + 16
    gain = norm_gain[0].astype(F32)[:, None]
    a_flat = adapter_a[0].reshape(adapters * rank, cols)
    b_flat = adapter_b[0].reshape(adapters * rank, cols)
    a_turned, b_turned = a_flat.T, b_flat.T
    member, live = tables_of(seg_ids, live_counts, adapters)
    block = exchange(base_weight[0].reshape(XS, width // XS, cols), ALONG_X)
    turned = block.transpose(0, 2, 1)
    block = block.reshape(XS, YS, CS, cols, cols)
    tokens = tokens_in.reshape(total, cols).T
    target = jnp.where(live[None, :], cotangent.reshape(total, cols).T, jnp.zeros((), BF))
    store = pltpu.VMEM((adapters * rank, total), BF)
    payload = ((XS, tall, total), BF)
    single = ((1, tall, total), BF)
    main = ((cols, total), BF)
    wide = ((cols, total), F32)

    def is_at(at):
        return (section == at).astype(jnp.int32)

    never = jnp.zeros((), jnp.int32)
    last = is_at(3)

    def mid_call(body, name, weight, weight_spec, got, other, alt, scratch=()):
        block_of = pl.BlockSpec((1, tall, total), lambda i, c: (i, 0, 0))
        full = pl.BlockSpec((XS, tall, total), lambda i, c: (0, 0, 0))
        ins, specs = [got], [full]
        if body is mid_forward:
            ins, specs = ins + [other, weight], specs + [full, weight_spec]
        else:
            ins, specs = ins + [weight], specs + [weight_spec]
            if other is not None:
                ins, specs = ins + [other], specs + [block_of]
        if alt is not None:
            ins.append(alt)
            specs.append(pl.BlockSpec((1, tall, total), lambda i, c: (0, 0, 0)))
        flag = never if alt is None else last
        return pl.pallas_call(
            body,
            grid_spec=pltpu.PrefetchScalarGridSpec(
                num_scalar_prefetch=1,
                grid=(4,),
                in_specs=specs,
                out_specs=block_of,
                scratch_shapes=list(scratch),
            ),
            out_shape=jax.ShapeDtypeStruct(*payload),
            compiler_params=PARAMS,
            name=name,
        )(jnp.stack([core, flag]), *ins)

    def start_forward(at, received, older, alt=None, out=payload):
        flags = jnp.stack([is_at(at), never if alt is None else last])
        extra = [] if alt is None else [alt]
        return whole_call(
            pre_forward,
            "pre_forward",
            [main, out],
            [flags, received, older, gain, a_flat, member] + extra,
            scalars=1,
        )

    def product_forward(got, alt=None):
        return mid_call(
            mid_forward,
            "mid_forward",
            turned,
            pl.BlockSpec((1, cols, width // XS), lambda i, c: (i, 0, 0)),
            got,
            swap_cores(got),
            alt,
            [pltpu.VMEM((width // XS, total), BF)],
        )

    kept_outs = [main, wide, ((rank, total), F32), ((1, total), F32), ((rank, total), BF)]

    def end_forward(got, current, ahead=None):
        body, outs, ins = post_forward, kept_outs, [got, current, b_turned, member]
        if ahead is not None:
            body = post_forward_turn
            outs, ins = outs + [((XS * YS * CS, 16, total), BF)], ins + [ahead]
        return whole_call(
            functools.partial(body, width), "post_forward", outs, ins, scratch=[store]
        )

    def product_backward(got, alt=None):
        shape = (XS, 1, 1, cols, cols)
        other = mid_call(
            mid_backward_other,
            "mid_backward_other",
            block,
            pl.BlockSpec(shape, lambda i, c: (0, i, 1 - c[0], 0, 0)),
            got,
            None,
            None,
        )
        return mid_call(
            mid_backward_own,
            "mid_backward_own",
            block,
            pl.BlockSpec(shape, lambda i, c: (0, i, c[0], 0, 0)),
            got,
            swap_cores(other),
            alt,
        )

    def end_backward(got, grad, current, down_raw, inverse):
        return whole_call(
            functools.partial(post_backward, width),
            "post_backward",
            [main],
            [got, grad, current, a_turned, member, down_raw, inverse, gain],
            scratch=[store],
        )[0]

    def start_backward(at, received, older, frozen, alt=None, out=payload):
        flags = jnp.stack([is_at(at), never if alt is None else last])
        extra = [] if alt is None else [alt]
        return whole_call(
            pre_backward,
            "pre_backward",
            [main, out],
            [flags, received, older, frozen, b_flat, member] + extra,
            scalars=1,
        )

    def onward(value):
        return lax.ppermute(value, "section", [(i, i + 1) for i in range(3)])

    def back(value):
        return lax.ppermute(value, "section", [(i + 1, i) for i in range(3)])

    current, sent = start_forward(0, tokens, jnp.zeros_like(tokens))
    got = exchange(sent, ALONG_Y)
    (alt,) = whole_call(pre_target, "pre_target", [single], [target, b_flat, member])
    got = exchange(product_forward(got, alt), ALONG_X)
    outs = end_forward(got, current)
    received = onward(outs[0])
    last_sums = product_backward(got)
    current, sent = start_forward(1, received, current)
    got = exchange(sent, ALONG_Y)
    got = exchange(product_forward(got), ALONG_X)
    outs = end_forward(got, current)
    received = onward(outs[0])
    current, sent = start_forward(2, received, current, last_sums)
    got = exchange(sent, ALONG_Y)
    (ahead,) = whole_call(
        functools.partial(post_target, rank),
        "post_target",
        [wide],
        [got, a_turned, member, gain],
        scratch=[store],
    )
    ahead = back(ahead)
    got = exchange(product_forward(got), ALONG_X)
    result, frozen, down_raw, inverse, down, small = end_forward(got, current, ahead)
    received = onward(result)
    small = lax.all_to_all(small, "dp", 0, 0)
    grad, sent = whole_call(
        functools.partial(turn, width),
        "turn",
        [main, payload],
        [is_at(2).reshape(1), small, result, target, ahead, frozen, b_flat, member],
        scalars=1,
    )
    got = exchange(sent, ALONG_X)
    current, alt = start_forward(3, received, current, out=single)
    got = exchange(product_backward(got, alt), ALONG_Y)
    received = back(end_backward(got, grad, current, down_raw, inverse))
    last_product = product_forward(got)
    grad, sent = start_backward(1, received, grad, frozen, last_product)
    got = exchange(sent, ALONG_X)
    outs = end_forward(got, current)
    got = exchange(product_backward(got), ALONG_Y)
    received = back(end_backward(got, grad, current, down_raw, inverse))
    grad, sent = start_backward(0, received, grad, frozen, out=single)
    ranks = sent[0, cols : cols + rank].astype(F32)
    ranks = (ranks + lax.ppermute(ranks, "dp", SIBLING)).astype(BF)
    ranks = exchange(jnp.broadcast_to(ranks[None], (XS * YS,) + ranks.shape), ALONG_XY)
    result = jnp.where(last > 0, outs[0], result)
    inverse = jnp.where(last > 0, outs[3], inverse)
    down = jnp.where(last > 0, outs[4], down)
    (grad_b,) = whole_call(
        outer_up,
        "outer_up",
        [((adapters * rank, cols), F32)],
        [down, grad, member],
        scratch=[store],
    )
    (grad_a,) = whole_call(
        outer_down,
        "outer_down",
        [((adapters * rank, cols), F32)],
        [ranks, current, inverse, gain, member],
        scratch=[store],
    )
    section_out = result.T.reshape(1, micro, rows, cols)
    shape = (1, adapters, rank, cols)
    return section_out, grad_a.reshape(shape), grad_b.reshape(shape)


def solution(mesh):
    in_specs = (
        P(None, None, "dp"),
        P(None, None, "dp"),
        P("section", None, "dp"),
        P("section", "dp"),
        P("section", None, None, "dp"),
        P("section", None, None, "dp"),
        P(),
        P(),
    )
    out_specs = (
        P("section", None, None, "dp"),
        P("section", None, None, "dp"),
        P("section", None, None, "dp"),
    )
    return jax.shard_map(
        on_device, mesh=mesh, in_specs=in_specs, out_specs=out_specs, check_vma=False
    )
```

```python
import functools

import jax
import jax.numpy as jnp
from jax import lax
from jax.experimental import pallas as pl
from jax.experimental.pallas import tpu as pltpu
from jax.sharding import PartitionSpec as P

EPSILON = 1e-06
SCALING = 2.0
XS, YS, CS = 4, 4, 2
BF = jnp.bfloat16
F32 = jnp.float32
VM = pl.BlockSpec(memory_space=pltpu.VMEM)
SM = pl.BlockSpec(memory_space=pltpu.SMEM)
PARAMS = pltpu.CompilerParams(vmem_limit_bytes=48 << 20)


def place(x, y, c):
    return (x * YS + y) * CS + c


def partner(x, y, c, k):
    other = lambda v: (v ^ 1) if c == 0 else ((v + 1) % 4 if v % 2 else (v - 1) % 4)
    return (other(x) if k & 2 else x), (other(y) if k & 1 else y)


APART = [
    [place(x + 2 * i, y + 2 * j, c) for i in range(2) for j in range(2)]
    for x in range(2)
    for y in range(2)
    for c in range(CS)
]
BLOCKS = [
    [place(*partner(x, y, c, k), c) for k in range(4)]
    for x in range(0, XS, 2)
    for y in range(0, YS, 2)
    for c in range(CS)
]
ALONG_XY = [[place(x, y, c) for x in range(XS) for y in range(YS)] for c in range(CS)]
SIBLING = [(i, i ^ 1) for i in range(XS * YS * CS)]


def exchange(chunks, groups):
    return lax.all_to_all(chunks, "dp", 0, 0, axis_index_groups=groups)


def swap_cores(block):
    return lax.ppermute(block, "dp", SIBLING)


def tables_of(seg_ids, live_counts, adapters):
    micro, rows = seg_ids.shape
    labels = jnp.arange(adapters, dtype=jnp.int32)
    member = (seg_ids[:, None, :] == labels[None, :, None]).astype(jnp.int32)
    counts = jnp.sum(member, axis=2)
    before = (labels[:, None] < labels[None, :]).astype(jnp.int32)
    starts = jnp.sum(counts[:, :, None] * before[None], axis=1)
    row_start = jnp.sum(member * starts[:, :, None], axis=1)
    row_limit = jnp.sum(member * jnp.minimum(live_counts, counts)[:, :, None], axis=1)
    live = jnp.arange(rows, dtype=jnp.int32)[None] - row_start < row_limit
    whole = member.astype(F32).transpose(1, 0, 2).reshape(adapters, micro * rows)
    return whole, live.reshape(micro * rows)


def dot(left, right, dims=((1,), (0,))):
    return lax.dot_general(left, right, (dims, ((), ())), preferred_element_type=F32)


def tail_of(ranks, rows):
    high = rows.astype(BF).astype(F32)
    return jnp.concatenate([ranks, high, rows - high], axis=0).astype(BF)


def eight(*rows):
    index = lax.broadcasted_iota(jnp.int32, (8, rows[0].shape[1]), 0)
    total = jnp.zeros(index.shape, F32)
    for at, row in enumerate(rows):
        total = jnp.where(index == at, row, total)
    return total


def extras(chunks, cols, rank):
    total = chunks[0, cols:].astype(F32)
    for j in range(1, chunks.shape[0]):
        total = total + chunks[j, cols:].astype(F32)
    return total[:rank], total[rank : rank + 8] + total[rank + 8 :]


def mains(chunks, cols):
    total = chunks[0, :cols].astype(F32)
    for j in range(1, chunks.shape[0]):
        total = total + chunks[j, :cols].astype(F32)
    return total


def select_rank(parts, member, rank):
    total = None
    for a in range(member.shape[0]):
        part = parts[a * rank : (a + 1) * rank] * member[a : a + 1, :]
        total = part if total is None else total + part
    return total


def spread_rank(values, member, store):
    rank = values.shape[0]
    for a in range(member.shape[0]):
        store[a * rank : (a + 1) * rank] = (values * member[a : a + 1, :]).astype(BF)


def fill(sent, main, tail):
    cols = main.shape[0]
    for j in range(sent.shape[0]):
        sent[j, :cols] = main
        sent[j, cols:] = tail


def column_sum(left, right):
    return jnp.sum(left * right, axis=0, keepdims=True)


def pre_forward(current, gain, a_flat, member, sent):
    rank = a_flat.shape[0] // member.shape[0]
    values = current[...].astype(F32)
    scaled = (values * gain[...]).astype(BF)
    ranks = select_rank(dot(a_flat[...], scaled), member, rank)
    fill(sent, scaled, tail_of(ranks, eight(column_sum(values, values))))


def mid_forward(info, got, other, weight, sent, joined):
    cols, rank = weight.shape[2], got.shape[1] - weight.shape[2] - 16
    core = info[0]

    @pl.when(pl.program_id(0) == 0)
    def _():
        for y in range(YS):
            mine = pl.multiple_of((y * CS + core) * cols, cols)
            theirs = pl.multiple_of((y * CS + 1 - core) * cols, cols)
            joined[pl.ds(mine, cols)] = got[y, :cols]
            joined[pl.ds(theirs, cols)] = other[y, :cols]

    sent[0, :cols] = dot(weight[0].T, joined[...]).astype(BF)
    ranks, rows = extras(got, cols, rank)
    ranks_o, rows_o = extras(other, cols, rank)
    sent[0, cols:] = tail_of(ranks + ranks_o, rows + rows_o)


def finish(width, got, current, b_turned, member, result, frozen, down_raw, inverse, down, store):
    cols, rank = current.shape[0], down.shape[0]
    total = mains(got, cols)
    ranks, rows = extras(got, cols, rank)
    scale = lax.rsqrt(rows[0:1] / width + EPSILON)
    kept = (ranks * scale).astype(BF)
    spread_rank(kept.astype(F32), member, store)
    adapter = dot(b_turned[...], store[...])
    value = (current[...].astype(F32) + total * scale + SCALING * adapter).astype(BF)
    result[...] = value
    frozen[...] = total
    down_raw[...] = ranks
    inverse[...] = scale
    down[...] = kept
    return value, total


def post_forward(width, *refs):
    finish(width, *refs)


def post_forward_turn(width, target, ahead, b_flat, *refs):
    sent = refs[-2]
    member, rank = refs[3], refs[-3].shape[0]
    value, frozen = finish(width, *refs[:-2], refs[-1])
    ranks = select_rank(dot(b_flat[...], value), member, rank)
    values = value.astype(F32)
    early, late = target[...].astype(F32), ahead[...].astype(F32)
    rows = eight(
        column_sum(values, values),
        column_sum(values, late),
        column_sum(early, frozen),
        column_sum(late, frozen),
        column_sum(values, frozen),
    )
    fill(sent, value, tail_of(ranks, rows))


def pre_backward(grad, frozen, b_flat, member, sent):
    rank = b_flat.shape[0] // member.shape[0]
    kept = grad[...]
    ranks = select_rank(dot(b_flat[...], kept), member, rank)
    row = column_sum(kept.astype(F32), frozen[...])
    fill(sent, kept, tail_of(ranks, eight(row)))


def pre_plain(grad, b_flat, member, sent):
    rank = b_flat.shape[0] // member.shape[0]
    kept = grad[...]
    ranks = select_rank(dot(b_flat[...], kept), member, rank)
    fill(sent, kept, tail_of(ranks, jnp.zeros((8, kept.shape[1]), F32)))


def row_product(got, weight, cols):
    total = dot(weight[0, 0, 0], got[0, :cols])
    for j in range(1, XS):
        total = total + dot(weight[j, 0, 0], got[j, :cols])
    return total


def mid_backward_other(info, got, weight, sent):
    cols = weight.shape[-1]
    sent[0, :cols] = row_product(got, weight, cols).astype(BF)
    sent[0, cols:] = tail_of(*extras(got, cols, got.shape[1] - cols - 16))


def mid_backward_own(info, got, weight, other, sent):
    cols = weight.shape[-1]
    rank = got.shape[1] - cols - 16
    total = row_product(got, weight, cols) + other[0, :cols].astype(F32)
    sent[0, :cols] = total.astype(BF)
    ranks, rows = extras(got, cols, rank)
    ranks_o, rows_o = extras(other, cols, rank)
    sent[0, cols:] = tail_of(ranks + ranks_o, rows + rows_o)


def add_up(got, total, ranks):
    cols, rank = total.shape[0], ranks.shape[0]
    total[...] = mains(got, cols)
    ranks[...] = extras(got, cols, rank)[0]


def post_target(rank, got, a_turned, member, gain, ahead, store):
    cols = ahead.shape[0]
    ranks, _ = extras(got, cols, rank)
    spread_rank((SCALING * ranks).astype(BF).astype(F32), member, store)
    normed_grad = mains(got, cols) + dot(a_turned[...], store[...])
    ahead[...] = (gain[...] * normed_grad).astype(BF)


def step_back(
    width, grad, back, ranks, row, current, a_turned, member, down_raw, inverse, gain, store
):
    grad_down = (SCALING * ranks).astype(BF).astype(F32)
    spread_rank(grad_down, member, store)
    normed_grad = back + dot(a_turned[...], store[...])
    stat = (row + column_sum(grad_down, down_raw[...])) / width
    scale = inverse[...]
    return (
        grad
        + scale * gain[...] * normed_grad
        - current[...].astype(F32) * (scale * scale * scale * stat)
    ).astype(BF)


def post_backward(
    width, got, grad, current, a_turned, member, down_raw, inverse, gain, grad_in, store
):
    cols, rank = current.shape[0], down_raw.shape[0]
    ranks, rows = extras(got, cols, rank)
    grad_in[...] = step_back(
        width, grad[...].astype(F32), mains(got, cols), ranks, rows[0:1],
        current, a_turned, member, down_raw, inverse, gain, store,
    )


def post_turn(
    width, got, back_first, ranks_first, back_late, ranks_late, target, ahead, result,
    current, a_turned, member, down_raw, inverse, gain, grad, grad_in, store,
):
    cols, rank = current.shape[0], down_raw.shape[0]
    ranks, rows = extras(got, cols, rank)
    scale = lax.rsqrt(rows[0:1] / width + EPSILON)
    least = scale * scale * scale * (rows[1:2] / width)
    fresh = (
        target[...].astype(F32)
        + scale * ahead[...].astype(F32)
        - least * result[...].astype(F32)
    )
    kept = fresh.astype(BF)
    grad[...] = kept
    grad_in[...] = step_back(
        width,
        kept.astype(F32),
        back_first[...] + scale * back_late[...] - least * mains(got, cols),
        ranks_first[...] + scale * ranks_late[...] - least * ranks,
        rows[2:3] + scale * rows[3:4] - least * rows[4:5],
        current, a_turned, member, down_raw, inverse, gain, store,
    )


def ranks_of(grad, b_flat, member, ranks):
    ranks[...] = select_rank(dot(b_flat[...], grad[...]), member, ranks.shape[0])


def outer_up(down, grad, member, grad_b, store):
    spread_rank(SCALING * down[...].astype(F32), member, store)
    grad_b[...] = dot(store[...], grad[...], ((1,), (1,)))


def outer_down(got, current, inverse, gain, member, grad_a, store):
    ranks = got[0].astype(F32)
    for j in range(1, got.shape[0]):
        ranks = ranks + got[j].astype(F32)
    spread_rank((SCALING * ranks).astype(BF).astype(F32), member, store)
    normed = (current[...].astype(F32) * inverse[...] * gain[...]).astype(BF)
    grad_a[...] = dot(store[...], normed, ((1,), (1,)))


def cost(flops, arrays):
    return pl.CostEstimate(
        flops=int(flops),
        bytes_accessed=sum(x.size * x.dtype.itemsize for x in arrays),
        transcendentals=0,
    )


def whole_call(body, name, outs, ins, scratch=(), flops=4e8):
    return pl.pallas_call(
        body,
        out_shape=[jax.ShapeDtypeStruct(s, d) for s, d in outs],
        in_specs=[VM] * len(ins),
        out_specs=[VM] * len(outs),
        scratch_shapes=list(scratch),
        compiler_params=PARAMS,
        cost_estimate=cost(flops, ins),
        name=name,
    )(*ins)


def on_device(
    tokens_in, cotangent, base_weight, norm_gain, adapter_a, adapter_b, seg_ids, live_counts
):
    section = lax.axis_index("section")
    at = lax.axis_index("dp")
    at_x, at_y, core = at // (YS * CS), (at // CS) % YS, at % CS
    micro, rows, cols = tokens_in.shape
    total = micro * rows
    adapters, rank = adapter_a.shape[1:3]
    width = base_weight.shape[1]
    tall = cols + rank + 16
    gain = norm_gain[0].astype(F32)[:, None]
    a_flat = adapter_a[0].reshape(adapters * rank, cols)
    b_flat = adapter_b[0].reshape(adapters * rank, cols)
    a_turned, b_turned = a_flat.T, b_flat.T
    member, live = tables_of(seg_ids, live_counts, adapters)
    info = core.astype(jnp.int32).reshape(1)
    store = pltpu.VMEM((adapters * rank, total), BF)
    payload = ((XS, tall, total), BF)
    main = ((cols, total), BF)
    wide = ((cols, total), F32)
    thin = ((rank, total), F32)
    kept_outs = [main, wide, thin, ((1, total), F32), ((rank, total), BF)]

    block = base_weight[0].reshape(2, 2, 2, 2, CS * cols, cols).transpose(1, 3, 0, 2, 4, 5)
    block = exchange(block.reshape(XS, width // XS, cols), BLOCKS)
    halves = block.reshape(XS, YS, CS, cols, cols)
    tokens = tokens_in.reshape(total, cols).T
    target = jnp.where(live[None, :], cotangent.reshape(total, cols).T, jnp.zeros((), BF))

    def mid_call(body, name, weight, weight_spec, ins, whole, scratch=(), flops=8e8):
        block_of = pl.BlockSpec((1, tall, total), lambda i, c: (i, 0, 0))
        full = pl.BlockSpec((XS, tall, total), lambda i, c: (0, 0, 0))
        specs = [full] * whole + [weight_spec] + [block_of] * (len(ins) - whole)
        ins = ins[:whole] + [weight] + ins[whole:]
        return pl.pallas_call(
            body,
            grid_spec=pltpu.PrefetchScalarGridSpec(
                num_scalar_prefetch=1,
                grid=(4,),
                in_specs=specs,
                out_specs=block_of,
                scratch_shapes=list(scratch),
            ),
            out_shape=jax.ShapeDtypeStruct(*payload),
            compiler_params=PARAMS,
            cost_estimate=cost(flops, ins),
            name=name,
        )(info, *ins)

    def start_forward(current, out=payload):
        (sent,) = whole_call(pre_forward, "pre_forward", [out], [current, gain, a_flat, member])
        return sent

    def product_forward(got, other):
        return mid_call(
            mid_forward,
            "mid_forward",
            block,
            pl.BlockSpec((1, width // XS, cols), lambda i, c: (i, 0, 0)),
            [got, other],
            2,
            [pltpu.VMEM((width // XS, total), BF)],
            flops=16e8,
        )

    def end_forward(got, current):
        return whole_call(
            functools.partial(post_forward, width),
            "post_forward",
            kept_outs,
            [got, current, b_turned, member],
            scratch=[store],
        )

    def forward(current):
        got = exchange(start_forward(current), APART)
        return exchange(product_forward(got, swap_cores(got)), BLOCKS)

    def product_backward(got):
        shape = (XS, 1, 1, cols, cols)
        other = mid_call(
            mid_backward_other,
            "mid_backward_other",
            halves,
            pl.BlockSpec(shape, lambda i, c: (0, i, 1 - c[0], 0, 0)),
            [got],
            1,
        )
        return mid_call(
            mid_backward_own,
            "mid_backward_own",
            halves,
            pl.BlockSpec(shape, lambda i, c: (0, i, c[0], 0, 0)),
            [got, swap_cores(other)],
            1,
        )

    def backward(got):
        return exchange(product_backward(got), APART)

    def plain(vector, out=payload):
        return whole_call(pre_plain, "pre_plain", [out], [vector, b_flat, member])[0]

    def sums_of(got):
        return whole_call(add_up, "add_up", [wide, thin], [backward(got)])

    def zeros(*kinds):
        return [jnp.zeros(*kind) for kind in kinds]

    def hop(value, pairs):
        return lax.ppermute(value, "section", pairs)

    def switch(cases, outs):
        nothing = lambda: tuple(zeros(*outs))
        return lax.switch(
            section, [(lambda f=cases.get(s): tuple(f())) if s in cases else nothing for s in range(4)]
        )

    single = ((1, tall, total), BF)
    gather = section < 2
    first = jnp.where(gather, start_forward(tokens, single), plain(target, single))
    turns = [first]
    for k in range(1, 4):
        pairs = []
        for i in range(4 * XS * YS * CS):
            s, x, y, c = i // (XS * YS * CS), i // (YS * CS) % XS, i // CS % YS, i % CS
            to = (x ^ (k & 2), y ^ (k & 1) * 2) if s < 2 else partner(x, y, c, k)
            pairs.append((i, s * XS * YS * CS + place(*to, c)))
        turns.append(lax.ppermute(first, ("section", "dp"), pairs))
    turns = jnp.concatenate(turns)
    own = jnp.where(gather, at_x // 2 * 2 + at_y // 2, at_x % 2 * 2 + at_y % 2)
    got = jnp.stack([lax.dynamic_index_in_dim(turns, own ^ j, 0, False) for j in range(4)])
    other = swap_cores(got)

    def run_first():
        outs = end_forward(exchange(product_forward(got, other), BLOCKS), tokens)
        return [outs[0], outs[3], outs[4]] + zeros(wide, thin)

    def run_target():
        (ahead,) = whole_call(
            functools.partial(post_target, rank),
            "post_target",
            [main],
            [backward(got), a_turned, member, gain],
            scratch=[store],
        )
        return [ahead] + zeros(kept_outs[3], kept_outs[4], wide, thin)

    def run_ready():
        return zeros(main, kept_outs[3], kept_outs[4]) + list(sums_of(got))

    vector, inverse_0, down_0, back_first, ranks_first = switch(
        {0: run_first, 3: run_target, 2: run_ready}, [main, kept_outs[3], kept_outs[4], wide, thin]
    )
    received = hop(vector, [(0, 1), (3, 2)])

    def run_second():
        return list(end_forward(forward(received), received)) + zeros(wide, thin)

    def run_late():
        return zeros(*kept_outs) + list(sums_of(exchange(plain(received), BLOCKS)))

    result_1, frozen_1, raw_1, inverse_1, down_1, back_late, ranks_late = switch(
        {1: run_second, 2: run_late}, kept_outs + [wide, thin]
    )
    second = hop(result_1, [(1, 2)])

    def run_turn():
        result, _, raw, inverse, down, sent = whole_call(
            functools.partial(post_forward_turn, width),
            "post_forward_turn",
            kept_outs + [payload],
            [target, received, b_flat, forward(second), second, b_turned, member],
            scratch=[store],
        )
        grad, grad_in = whole_call(
            functools.partial(post_turn, width),
            "post_turn",
            [main, main],
            [backward(exchange(sent, BLOCKS)), back_first, ranks_first, back_late, ranks_late, target, received]
            + [result, second, a_turned, member, raw, inverse, gain],
            scratch=[store],
        )
        return result, inverse, down, grad, grad_in

    result_2, inverse_2, down_2, grad_2, grad_in = switch(
        {2: run_turn}, [main, kept_outs[3], kept_outs[4], main, main]
    )
    third = hop(result_2, [(2, 3)])
    grad_1 = hop(grad_in, [(2, 1)])

    def run_back():
        (sent,) = whole_call(
            pre_backward, "pre_backward", [payload], [grad_1, frozen_1, b_flat, member]
        )
        (grad_in,) = whole_call(
            functools.partial(post_backward, width),
            "post_backward",
            [main],
            [backward(exchange(sent, BLOCKS)), grad_1, received, a_turned, member, raw_1, inverse_1, gain],
            scratch=[store],
        )
        return [grad_in] + zeros(kept_outs[3], kept_outs[4])

    def run_last():
        outs = end_forward(forward(third), third)
        return outs[0], outs[3], outs[4]

    vector_3, inverse_3, down_3 = switch({1: run_back, 3: run_last}, [main] + kept_outs[3:])
    grad_0 = hop(vector_3, [(1, 0)])

    def choose(*values):
        return lax.select_n(section.astype(jnp.int32), *values)

    grad = choose(grad_0, grad_1, grad_2, target)
    (ranks,) = whole_call(ranks_of, "ranks_of", [thin], [grad, b_flat, member])
    ranks = (ranks + swap_cores(ranks)).astype(BF)
    ranks = exchange(jnp.broadcast_to(ranks[None], (XS * YS,) + ranks.shape), ALONG_XY)
    current = choose(tokens, received, second, third)
    result = choose(vector, result_1, result_2, vector_3)
    inverse = choose(inverse_0, inverse_1, inverse_2, inverse_3)
    down = choose(down_0, down_1, down_2, down_3)
    (grad_b,) = whole_call(
        outer_up,
        "outer_up",
        [((adapters * rank, cols), F32)],
        [down, grad, member],
        scratch=[store],
    )
    (grad_a,) = whole_call(
        outer_down,
        "outer_down",
        [((adapters * rank, cols), F32)],
        [ranks, current, inverse, gain, member],
        scratch=[store],
    )
    section_out = result.T.reshape(1, micro, rows, cols)
    shape = (1, adapters, rank, cols)
    return section_out, grad_a.reshape(shape), grad_b.reshape(shape)


def solution(mesh):
    in_specs = (
        P(None, None, "dp"),
        P(None, None, "dp"),
        P("section", None, "dp"),
        P("section", "dp"),
        P("section", None, None, "dp"),
        P("section", None, None, "dp"),
        P(),
        P(),
    )
    out_specs = (
        P("section", None, None, "dp"),
        P("section", None, None, "dp"),
        P("section", None, None, "dp"),
    )
    return jax.shard_map(
        on_device, mesh=mesh, in_specs=in_specs, out_specs=out_specs, check_vma=False
    )
```

```python
import functools

import jax
import jax.numpy as jnp
from jax import lax
from jax.experimental import pallas as pl
from jax.experimental.pallas import tpu as pltpu
from jax.sharding import PartitionSpec as P

EPSILON = 1e-06
SCALING = 2.0
XS, YS, CS = 4, 4, 2
BF = jnp.bfloat16
F32 = jnp.float32
VM = pl.BlockSpec(memory_space=pltpu.VMEM)
SM = pl.BlockSpec(memory_space=pltpu.SMEM)
PARAMS = pltpu.CompilerParams(vmem_limit_bytes=24 << 20)


def place(x, y, c):
    return (x * YS + y) * CS + c


def partner(x, y, c, k):
    other = lambda v: (v ^ 1) if c == 0 else ((v + 1) % 4 if v % 2 else (v - 1) % 4)
    return (other(x) if k & 2 else x), (other(y) if k & 1 else y)


APART = [
    [place(x + 2 * i, y + 2 * j, c) for i in range(2) for j in range(2)]
    for x in range(2)
    for y in range(2)
    for c in range(CS)
]
BLOCKS = [
    [place(*partner(x, y, c, k), c) for k in range(4)]
    for x in range(0, XS, 2)
    for y in range(0, YS, 2)
    for c in range(CS)
]
ALONG_XY = [[place(x, y, c) for x in range(XS) for y in range(YS)] for c in range(CS)]
SIBLING = [(i, i ^ 1) for i in range(XS * YS * CS)]


def exchange(chunks, groups):
    return lax.all_to_all(chunks, "dp", 0, 0, axis_index_groups=groups)


def swap_cores(block):
    return lax.ppermute(block, "dp", SIBLING)


def tables_of(seg_ids, live_counts, adapters):
    micro, rows = seg_ids.shape
    labels = jnp.arange(adapters, dtype=jnp.int32)
    member = (seg_ids[:, None, :] == labels[None, :, None]).astype(jnp.int32)
    counts = jnp.sum(member, axis=2)
    before = (labels[:, None] < labels[None, :]).astype(jnp.int32)
    starts = jnp.sum(counts[:, :, None] * before[None], axis=1)
    row_start = jnp.sum(member * starts[:, :, None], axis=1)
    row_limit = jnp.sum(member * jnp.minimum(live_counts, counts)[:, :, None], axis=1)
    live = jnp.arange(rows, dtype=jnp.int32)[None] - row_start < row_limit
    whole = member.astype(F32).transpose(1, 0, 2).reshape(adapters, micro * rows)
    return whole, live.reshape(micro * rows)


def dot(left, right, dims=((1,), (0,))):
    return lax.dot_general(left, right, (dims, ((), ())), preferred_element_type=F32)


def tail_of(ranks, rows):
    high = rows.astype(BF).astype(F32)
    return jnp.concatenate([ranks, high, rows - high], axis=0).astype(BF)


def eight(*rows):
    index = lax.broadcasted_iota(jnp.int32, (8, rows[0].shape[1]), 0)
    total = jnp.zeros(index.shape, F32)
    for at, row in enumerate(rows):
        total = jnp.where(index == at, row, total)
    return total


def extras(chunks, cols, rank):
    total = chunks[0, cols:].astype(F32)
    for j in range(1, chunks.shape[0]):
        total = total + chunks[j, cols:].astype(F32)
    return total[:rank], total[rank : rank + 8] + total[rank + 8 :]


def mains(chunks, cols):
    total = chunks[0, :cols].astype(F32)
    for j in range(1, chunks.shape[0]):
        total = total + chunks[j, :cols].astype(F32)
    return total


def select_rank(parts, member, rank):
    total = None
    for a in range(member.shape[0]):
        part = parts[a * rank : (a + 1) * rank] * member[a : a + 1, :]
        total = part if total is None else total + part
    return total


def spread_rank(values, member, store):
    rank = values.shape[0]
    for a in range(member.shape[0]):
        store[a * rank : (a + 1) * rank] = (values * member[a : a + 1, :]).astype(BF)


def fill(sent, main, tail):
    cols = main.shape[0]
    for j in range(sent.shape[0]):
        sent[j, :cols] = main
        sent[j, cols:] = tail


def column_sum(left, right):
    return jnp.sum(left * right, axis=0, keepdims=True)


def pre_forward(current, gain, a_flat, member, sent):
    rank = a_flat.shape[0] // member.shape[0]
    values = current[...].astype(F32)
    scaled = (values * gain[...]).astype(BF)
    ranks = select_rank(dot(a_flat[...], scaled), member, rank)
    fill(sent, scaled, tail_of(ranks, eight(column_sum(values, values))))


def turn_rows(got, cols, turned):
    @pl.when(pl.program_id(0) == 0)
    def _():
        turned[...] = got[:, :cols].reshape(got.shape[0] * cols, got.shape[2]).T


def mid_forward_own(info, got, weight, total, turned):
    cols = weight.shape[-1]
    turn_rows(got, cols, turned)
    for i in range(total.shape[0]):
        total[i] = dot(turned[...], weight[i].reshape(YS * cols, cols))


def mid_forward(info, got, other, weight, total, sent, turned):
    cols = weight.shape[-1]
    rank = got.shape[1] - cols - 16
    turn_rows(other, cols, turned)
    ranks, rows = extras(got, cols, rank)
    ranks_o, rows_o = extras(other, cols, rank)
    tail = tail_of(ranks + ranks_o, rows + rows_o)
    for i in range(sent.shape[0]):
        both = total[i] + dot(turned[...], weight[i].reshape(YS * cols, cols))
        sent[i, :cols] = both.astype(BF).T
        sent[i, cols:] = tail


def finish(width, got, current, b_turned, member, result, frozen, down_raw, inverse, down, store):
    cols, rank = current.shape[0], down.shape[0]
    total = mains(got, cols)
    ranks, rows = extras(got, cols, rank)
    scale = lax.rsqrt(rows[0:1] / width + EPSILON)
    kept = (ranks * scale).astype(BF)
    spread_rank(kept.astype(F32), member, store)
    adapter = dot(b_turned[...], store[...])
    value = (current[...].astype(F32) + total * scale + SCALING * adapter).astype(BF)
    result[...] = value
    frozen[...] = total
    down_raw[...] = ranks
    inverse[...] = scale
    down[...] = kept
    return value, total


def post_forward(width, *refs):
    finish(width, *refs)


def post_forward_turn(width, target, ahead, b_flat, *refs):
    sent = refs[-2]
    member, rank = refs[3], refs[-3].shape[0]
    value, frozen = finish(width, *refs[:-2], refs[-1])
    ranks = select_rank(dot(b_flat[...], value), member, rank)
    values = value.astype(F32)
    early, late = target[...].astype(F32), ahead[...].astype(F32)
    rows = eight(
        column_sum(values, values),
        column_sum(values, late),
        column_sum(early, frozen),
        column_sum(late, frozen),
        column_sum(values, frozen),
    )
    fill(sent, value, tail_of(ranks, rows))


def pre_backward(grad, frozen, b_flat, member, sent):
    rank = b_flat.shape[0] // member.shape[0]
    kept = grad[...]
    ranks = select_rank(dot(b_flat[...], kept), member, rank)
    row = column_sum(kept.astype(F32), frozen[...])
    fill(sent, kept, tail_of(ranks, eight(row)))


def pre_plain(grad, b_flat, member, sent):
    rank = b_flat.shape[0] // member.shape[0]
    kept = grad[...]
    ranks = select_rank(dot(b_flat[...], kept), member, rank)
    fill(sent, kept, tail_of(ranks, jnp.zeros((8, kept.shape[1]), F32)))


def row_product(got, weight):
    chips, cols = weight.shape[1], weight.shape[-1]
    total = None
    for j in range(XS):
        part = dot(weight[j].reshape(chips * cols, cols), got[j, :cols])
        total = part if total is None else total + part
    return total.reshape(chips, cols, total.shape[1])


def mid_backward_other(info, got, weight, sent):
    cols = weight.shape[-1]
    main = row_product(got, weight).astype(BF)
    tail = tail_of(*extras(got, cols, got.shape[1] - cols - 16))
    for j in range(sent.shape[0]):
        sent[j, :cols] = main[j]
        sent[j, cols:] = tail


def mid_backward_own(info, got, weight, total):
    total[...] = row_product(got, weight)


def mid_backward(got, total, other, sent):
    cols = total.shape[1]
    rank = got.shape[1] - cols - 16
    ranks, rows = extras(got, cols, rank)
    ranks_o, rows_o = extras(other[:1], cols, rank)
    tail = tail_of(ranks + ranks_o, rows + rows_o)
    for j in range(sent.shape[0]):
        sent[j, :cols] = (total[j] + other[j, :cols].astype(F32)).astype(BF)
        sent[j, cols:] = tail


def add_up(got, total, ranks):
    cols, rank = total.shape[0], ranks.shape[0]
    total[...] = mains(got, cols)
    ranks[...] = extras(got, cols, rank)[0]


def post_target(rank, got, a_turned, member, gain, ahead, store):
    cols = ahead.shape[0]
    ranks, _ = extras(got, cols, rank)
    spread_rank((SCALING * ranks).astype(BF).astype(F32), member, store)
    normed_grad = mains(got, cols) + dot(a_turned[...], store[...])
    ahead[...] = (gain[...] * normed_grad).astype(BF)


def step_back(
    width, grad, back, ranks, row, current, a_turned, member, down_raw, inverse, gain, store
):
    grad_down = (SCALING * ranks).astype(BF).astype(F32)
    spread_rank(grad_down, member, store)
    normed_grad = back + dot(a_turned[...], store[...])
    stat = (row + column_sum(grad_down, down_raw[...])) / width
    scale = inverse[...]
    return (
        grad
        + scale * gain[...] * normed_grad
        - current[...].astype(F32) * (scale * scale * scale * stat)
    ).astype(BF)


def post_backward(
    width, got, grad, current, a_turned, member, down_raw, inverse, gain, grad_in, store
):
    cols, rank = current.shape[0], down_raw.shape[0]
    ranks, rows = extras(got, cols, rank)
    grad_in[...] = step_back(
        width, grad[...].astype(F32), mains(got, cols), ranks, rows[0:1],
        current, a_turned, member, down_raw, inverse, gain, store,
    )


def post_turn(
    width, got, back_first, ranks_first, back_late, ranks_late, target, ahead, result,
    current, a_turned, member, down_raw, inverse, gain, grad, grad_in, store,
):
    cols, rank = current.shape[0], down_raw.shape[0]
    ranks, rows = extras(got, cols, rank)
    scale = lax.rsqrt(rows[0:1] / width + EPSILON)
    least = scale * scale * scale * (rows[1:2] / width)
    fresh = (
        target[...].astype(F32)
        + scale * ahead[...].astype(F32)
        - least * result[...].astype(F32)
    )
    kept = fresh.astype(BF)
    grad[...] = kept
    grad_in[...] = step_back(
        width,
        kept.astype(F32),
        back_first[...] + scale * back_late[...] - least * mains(got, cols),
        ranks_first[...] + scale * ranks_late[...] - least * ranks,
        rows[2:3] + scale * rows[3:4] - least * rows[4:5],
        current, a_turned, member, down_raw, inverse, gain, store,
    )


def ranks_of(flag, received, others, b_flat, member, grad, ranks):
    kept = jnp.where(flag[0] > 0, received[...].astype(F32), others[...].astype(F32)).astype(BF)
    grad[...] = kept
    ranks[...] = select_rank(dot(b_flat[...], kept), member, ranks.shape[0])


def outer_up(down, grad, member, grad_b, store):
    spread_rank(SCALING * down[...].astype(F32), member, store)
    grad_b[...] = dot(store[...], grad[...], ((1,), (1,)))


def outer_down(got, current, inverse, gain, member, grad_a, store):
    ranks = got[0].astype(F32)
    for j in range(1, got.shape[0]):
        ranks = ranks + got[j].astype(F32)
    spread_rank((SCALING * ranks).astype(BF).astype(F32), member, store)
    normed = (current[...].astype(F32) * inverse[...] * gain[...]).astype(BF)
    grad_a[...] = dot(store[...], normed, ((1,), (1,)))


def cost(flops, arrays):
    return pl.CostEstimate(
        flops=int(flops),
        bytes_accessed=sum(x.size * x.dtype.itemsize for x in arrays),
        transcendentals=0,
    )


def whole_call(body, name, outs, ins, scratch=(), flops=4e8, scalars=0):
    return pl.pallas_call(
        body,
        out_shape=[jax.ShapeDtypeStruct(s, d) for s, d in outs],
        in_specs=[SM] * scalars + [VM] * (len(ins) - scalars),
        out_specs=[VM] * len(outs),
        scratch_shapes=list(scratch),
        compiler_params=PARAMS,
        cost_estimate=cost(flops, ins),
        name=name,
    )(*ins)


def on_device(
    tokens_in, cotangent, base_weight, norm_gain, adapter_a, adapter_b, seg_ids, live_counts
):
    section = lax.axis_index("section")
    at = lax.axis_index("dp")
    at_x, at_y, core = at // (YS * CS), (at // CS) % YS, at % CS
    micro, rows, cols = tokens_in.shape
    total = micro * rows
    adapters, rank = adapter_a.shape[1:3]
    width = base_weight.shape[1]
    tall = cols + rank + 16
    gain = norm_gain[0].astype(F32)[:, None]
    a_flat = adapter_a[0].reshape(adapters * rank, cols)
    b_flat = adapter_b[0].reshape(adapters * rank, cols)
    a_turned, b_turned = a_flat.T, b_flat.T
    member, live = tables_of(seg_ids, live_counts, adapters)
    info = core.astype(jnp.int32).reshape(1)
    store = pltpu.VMEM((adapters * rank, total), BF)
    payload = ((XS, tall, total), BF)
    main = ((cols, total), BF)
    wide = ((cols, total), F32)
    thin = ((rank, total), F32)
    kept_outs = [main, wide, thin, ((1, total), F32), ((rank, total), BF)]

    block = base_weight[0].reshape(2, 2, 2, 2, CS * cols, cols).transpose(1, 3, 0, 2, 4, 5)
    block = exchange(block.reshape(XS, width // XS, cols), BLOCKS)
    halves = block.reshape(XS, YS, CS, cols, cols)
    tokens = tokens_in.reshape(total, cols).T
    target = jnp.where(live[None, :], cotangent.reshape(total, cols).T, jnp.zeros((), BF))

    def mid_call(body, name, steps, specs, ins, out, out_rows, flops, scratch=()):
        return pl.pallas_call(
            body,
            grid_spec=pltpu.PrefetchScalarGridSpec(
                num_scalar_prefetch=1,
                grid=(steps,),
                in_specs=specs,
                out_specs=pl.BlockSpec((XS // steps,) + out_rows, lambda i, c: (i, 0, 0)),
                scratch_shapes=list(scratch),
            ),
            out_shape=jax.ShapeDtypeStruct((XS,) + out_rows, out),
            compiler_params=PARAMS,
            cost_estimate=cost(flops, ins),
            name=name,
        )(info, *ins)

    tall_full = pl.BlockSpec((XS, tall, total), lambda i, c: (0, 0, 0))

    def start_forward(current, out=payload):
        (sent,) = whole_call(pre_forward, "pre_forward", [out], [current, gain, a_flat, member])
        return sent

    def product_forward(got):
        shape = (2, YS, 1, cols, cols)
        other = swap_cores(got)
        own = mid_call(
            mid_forward_own,
            "mid_forward_own",
            2,
            [tall_full, pl.BlockSpec(shape, lambda i, c: (i, 0, c[0], 0, 0))],
            [got, halves],
            F32,
            (total, cols),
            8e8,
            [pltpu.VMEM((total, YS * cols), BF)],
        )
        return mid_call(
            mid_forward,
            "mid_forward",
            2,
            [
                tall_full,
                tall_full,
                pl.BlockSpec(shape, lambda i, c: (i, 0, 1 - c[0], 0, 0)),
                pl.BlockSpec((2, total, cols), lambda i, c: (i, 0, 0)),
            ],
            [got, other, halves, own],
            BF,
            (tall, total),
            8e8,
            [pltpu.VMEM((total, YS * cols), BF)],
        )

    def end_forward(got, current):
        return whole_call(
            functools.partial(post_forward, width),
            "post_forward",
            kept_outs,
            [got, current, b_turned, member],
            scratch=[store],
        )

    def forward(current):
        got = exchange(start_forward(current), APART)
        return exchange(product_forward(got), BLOCKS)

    def product_backward(got):
        shape = (XS, 2, 1, cols, cols)
        other = mid_call(
            mid_backward_other,
            "mid_backward_other",
            2,
            [tall_full, pl.BlockSpec(shape, lambda i, c: (0, i, 1 - c[0], 0, 0))],
            [got, halves],
            BF,
            (tall, total),
            8e8,
        )
        own = mid_call(
            mid_backward_own,
            "mid_backward_own",
            2,
            [tall_full, pl.BlockSpec(shape, lambda i, c: (0, i, c[0], 0, 0))],
            [got, halves],
            F32,
            (cols, total),
            8e8,
        )
        (sent,) = whole_call(
            mid_backward, "mid_backward", [payload], [got, own, swap_cores(other)], flops=1e6
        )
        return sent

    def backward(got):
        return exchange(product_backward(got), APART)

    def plain(vector, out=payload):
        return whole_call(pre_plain, "pre_plain", [out], [vector, b_flat, member])[0]

    def sums_of(got):
        return whole_call(add_up, "add_up", [wide, thin], [backward(got)])

    def zeros(*kinds):
        return [jnp.zeros(*kind) for kind in kinds]

    def hop(value, pairs):
        return lax.ppermute(value, "section", pairs)

    def switch(cases, outs):
        nothing = lambda: tuple(zeros(*outs))
        return lax.switch(
            section, [(lambda f=cases.get(s): tuple(f())) if s in cases else nothing for s in range(4)]
        )

    single = ((1, tall, total), BF)
    gather = section < 2
    first = jnp.where(gather, start_forward(tokens, single), plain(target, single))
    turns = [first]
    for k in range(1, 4):
        pairs = []
        for i in range(4 * XS * YS * CS):
            s, x, y, c = i // (XS * YS * CS), i // (YS * CS) % XS, i // CS % YS, i % CS
            to = (x ^ (k & 2), y ^ (k & 1) * 2) if s < 2 else partner(x, y, c, k)
            pairs.append((i, s * XS * YS * CS + place(*to, c)))
        turns.append(lax.ppermute(first, ("section", "dp"), pairs))
    turns = jnp.concatenate(turns)
    own = jnp.where(gather, at_x // 2 * 2 + at_y // 2, at_x % 2 * 2 + at_y % 2)
    got = jnp.stack([lax.dynamic_index_in_dim(turns, own ^ j, 0, False) for j in range(4)])

    def run_first():
        outs = end_forward(exchange(product_forward(got), BLOCKS), tokens)
        return [outs[0], outs[3], outs[4]] + zeros(wide, thin)

    def run_target():
        (ahead,) = whole_call(
            functools.partial(post_target, rank),
            "post_target",
            [main],
            [backward(got), a_turned, member, gain],
            scratch=[store],
        )
        return [ahead] + zeros(kept_outs[3], kept_outs[4], wide, thin)

    def run_ready():
        return zeros(main, kept_outs[3], kept_outs[4]) + list(sums_of(got))

    vector, inverse_0, down_0, back_first, ranks_first = switch(
        {0: run_first, 3: run_target, 2: run_ready}, [main, kept_outs[3], kept_outs[4], wide, thin]
    )
    received = hop(vector, [(0, 1), (3, 2)])

    def run_second():
        return list(end_forward(forward(received), received)) + zeros(wide, thin)

    def run_late():
        return zeros(*kept_outs) + list(sums_of(exchange(plain(received), BLOCKS)))

    result_1, frozen_1, raw_1, inverse_1, down_1, back_late, ranks_late = switch(
        {1: run_second, 2: run_late}, kept_outs + [wide, thin]
    )
    second = hop(result_1, [(1, 2)])

    def run_turn():
        result, _, raw, inverse, down, sent = whole_call(
            functools.partial(post_forward_turn, width),
            "post_forward_turn",
            kept_outs + [payload],
            [target, received, b_flat, forward(second), second, b_turned, member],
            scratch=[store],
        )
        grad, grad_in = whole_call(
            functools.partial(post_turn, width),
            "post_turn",
            [main, main],
            [backward(exchange(sent, BLOCKS)), back_first, ranks_first, back_late, ranks_late, target, received]
            + [result, second, a_turned, member, raw, inverse, gain],
            scratch=[store],
        )
        return result, inverse, down, grad, grad_in

    result_2, inverse_2, down_2, grad_2, grad_in = switch(
        {2: run_turn}, [main, kept_outs[3], kept_outs[4], main, main]
    )
    third = hop(result_2, [(2, 3)])
    grad_1 = hop(grad_in, [(2, 1)])

    def run_back():
        (sent,) = whole_call(
            pre_backward, "pre_backward", [payload], [grad_1, frozen_1, b_flat, member]
        )
        (grad_in,) = whole_call(
            functools.partial(post_backward, width),
            "post_backward",
            [main],
            [backward(exchange(sent, BLOCKS)), grad_1, received, a_turned, member, raw_1, inverse_1, gain],
            scratch=[store],
        )
        return [grad_in] + zeros(kept_outs[3], kept_outs[4])

    def run_last():
        outs = end_forward(forward(third), third)
        return outs[0], outs[3], outs[4]

    vector_3, inverse_3, down_3 = switch({1: run_back, 3: run_last}, [main] + kept_outs[3:])
    grad_0 = hop(vector_3, [(1, 0)])

    def choose(*values):
        return lax.select_n(section.astype(jnp.int32), *values)

    others = choose(target, grad_1, grad_2, target)
    grad, ranks = whole_call(
        ranks_of,
        "ranks_of",
        [main, thin],
        [(section == 0).astype(jnp.int32).reshape(1), grad_0, others, b_flat, member],
        scalars=1,
    )
    ranks = (ranks + swap_cores(ranks)).astype(BF)
    ranks = exchange(jnp.broadcast_to(ranks[None], (XS * YS,) + ranks.shape), ALONG_XY)
    current = choose(tokens, received, second, third)
    result = choose(vector, result_1, result_2, vector_3)
    inverse = choose(inverse_0, inverse_1, inverse_2, inverse_3)
    down = choose(down_0, down_1, down_2, down_3)
    (grad_b,) = whole_call(
        outer_up,
        "outer_up",
        [((adapters * rank, cols), F32)],
        [down, grad, member],
        scratch=[store],
    )
    (grad_a,) = whole_call(
        outer_down,
        "outer_down",
        [((adapters * rank, cols), F32)],
        [ranks, current, inverse, gain, member],
        scratch=[store],
    )
    section_out = result.T.reshape(1, micro, rows, cols)
    shape = (1, adapters, rank, cols)
    return section_out, grad_a.reshape(shape), grad_b.reshape(shape)


def solution(mesh):
    in_specs = (
        P(None, None, "dp"),
        P(None, None, "dp"),
        P("section", None, "dp"),
        P("section", "dp"),
        P("section", None, None, "dp"),
        P("section", None, None, "dp"),
        P(),
        P(),
    )
    out_specs = (
        P("section", None, None, "dp"),
        P("section", None, None, "dp"),
        P("section", None, None, "dp"),
    )
    return jax.shard_map(
        on_device, mesh=mesh, in_specs=in_specs, out_specs=out_specs, check_vma=False
    )
```

```python
import functools

import jax
import jax.numpy as jnp
from jax import lax
from jax.experimental import pallas as pl
from jax.experimental.pallas import tpu as pltpu
from jax.sharding import PartitionSpec as P

EPSILON = 1e-06
SCALING = 2.0
XS, YS, CS = 4, 4, 2
BF = jnp.bfloat16
F32 = jnp.float32
VM = pl.BlockSpec(memory_space=pltpu.VMEM)
SM = pl.BlockSpec(memory_space=pltpu.SMEM)
PARAMS = pltpu.CompilerParams(vmem_limit_bytes=24 << 20)


def place(x, y, c):
    return (x * YS + y) * CS + c


def partner(x, y, c, k):
    other = lambda v: (v ^ 1) if c == 0 else ((v + 1) % 4 if v % 2 else (v - 1) % 4)
    return (other(x) if k & 2 else x), (other(y) if k & 1 else y)


APART = [
    [place(x + 2 * i, y + 2 * j, c) for i in range(2) for j in range(2)]
    for x in range(2)
    for y in range(2)
    for c in range(CS)
]
BLOCKS = [
    [place(*partner(x, y, c, k), c) for k in range(4)]
    for x in range(0, XS, 2)
    for y in range(0, YS, 2)
    for c in range(CS)
]
ALONG_XY = [[place(x, y, c) for x in range(XS) for y in range(YS)] for c in range(CS)]
SIBLING = [(i, i ^ 1) for i in range(XS * YS * CS)]


def exchange(chunks, groups):
    return lax.all_to_all(chunks, "dp", 0, 0, axis_index_groups=groups)


def swap_cores(block):
    return lax.ppermute(block, "dp", SIBLING)


def tables_of(seg_ids, live_counts, adapters):
    micro, rows = seg_ids.shape
    labels = jnp.arange(adapters, dtype=jnp.int32)
    member = (seg_ids[:, None, :] == labels[None, :, None]).astype(jnp.int32)
    counts = jnp.sum(member, axis=2)
    before = (labels[:, None] < labels[None, :]).astype(jnp.int32)
    starts = jnp.sum(counts[:, :, None] * before[None], axis=1)
    row_start = jnp.sum(member * starts[:, :, None], axis=1)
    row_limit = jnp.sum(member * jnp.minimum(live_counts, counts)[:, :, None], axis=1)
    live = jnp.arange(rows, dtype=jnp.int32)[None] - row_start < row_limit
    whole = member.astype(F32).transpose(1, 0, 2).reshape(adapters, micro * rows)
    return whole, live.reshape(micro * rows)


def dot(left, right, dims=((1,), (0,))):
    return lax.dot_general(left, right, (dims, ((), ())), preferred_element_type=F32)


def tail_of(ranks, rows):
    high = rows.astype(BF).astype(F32)
    return jnp.concatenate([ranks, high, rows - high], axis=0).astype(BF)


def eight(*rows):
    index = lax.broadcasted_iota(jnp.int32, (8, rows[0].shape[1]), 0)
    total = jnp.zeros(index.shape, F32)
    for at, row in enumerate(rows):
        total = jnp.where(index == at, row, total)
    return total


def extras(chunks, cols, rank):
    total = chunks[0, cols:].astype(F32)
    for j in range(1, chunks.shape[0]):
        total = total + chunks[j, cols:].astype(F32)
    return total[:rank], total[rank : rank + 8] + total[rank + 8 :]


def mains(chunks, cols):
    total = chunks[0, :cols].astype(F32)
    for j in range(1, chunks.shape[0]):
        total = total + chunks[j, :cols].astype(F32)
    return total


def select_rank(parts, member, rank):
    total = None
    for a in range(member.shape[0]):
        part = parts[a * rank : (a + 1) * rank] * member[a : a + 1, :]
        total = part if total is None else total + part
    return total


def spread_rank(values, member, store):
    rank = values.shape[0]
    for a in range(member.shape[0]):
        store[a * rank : (a + 1) * rank] = (values * member[a : a + 1, :]).astype(BF)


def fill(sent, main, tail):
    cols = main.shape[0]
    for j in range(sent.shape[0]):
        sent[j, :cols] = main
        sent[j, cols:] = tail


def column_sum(left, right):
    return jnp.sum(left * right, axis=0, keepdims=True)


def pre_forward(current, gain, a_flat, member, sent):
    rank = a_flat.shape[0] // member.shape[0]
    values = current[...].astype(F32)
    scaled = (values * gain[...]).astype(BF)
    ranks = select_rank(dot(a_flat[...], scaled), member, rank)
    fill(sent, scaled, tail_of(ranks, eight(column_sum(values, values))))


def turn_rows(got, cols, turned):
    @pl.when(pl.program_id(0) == 0)
    def _():
        turned[...] = got[:, :cols].reshape(got.shape[0] * cols, got.shape[2]).T


def mid_forward_own(info, got, weight, total, turned):
    cols = weight.shape[-1]
    turn_rows(got, cols, turned)
    for i in range(total.shape[0]):
        total[i] = dot(turned[...], weight[i].reshape(YS * cols, cols))


def mid_forward(info, got, other, weight, total, sent, turned):
    cols = weight.shape[-1]
    rank = got.shape[1] - cols - 16
    turn_rows(other, cols, turned)
    ranks, rows = extras(got, cols, rank)
    ranks_o, rows_o = extras(other, cols, rank)
    tail = tail_of(ranks + ranks_o, rows + rows_o)
    for i in range(sent.shape[0]):
        both = total[i] + dot(turned[...], weight[i].reshape(YS * cols, cols))
        sent[i, :cols] = both.astype(BF).T
        sent[i, cols:] = tail


def finish(width, got, current, b_turned, member, result, frozen, down_raw, inverse, down, store):
    cols, rank = current.shape[0], down.shape[0]
    total = mains(got, cols)
    ranks, rows = extras(got, cols, rank)
    scale = lax.rsqrt(rows[0:1] / width + EPSILON)
    kept = (ranks * scale).astype(BF)
    spread_rank(kept.astype(F32), member, store)
    adapter = dot(b_turned[...], store[...])
    value = (current[...].astype(F32) + total * scale + SCALING * adapter).astype(BF)
    result[...] = value
    frozen[...] = total
    down_raw[...] = ranks
    inverse[...] = scale
    down[...] = kept
    return value, total


def post_forward(width, *refs):
    finish(width, *refs)


def post_forward_turn(width, target, ahead, b_flat, *refs):
    sent = refs[-2]
    member, rank = refs[3], refs[-3].shape[0]
    value, frozen = finish(width, *refs[:-2], refs[-1])
    ranks = select_rank(dot(b_flat[...], value), member, rank)
    values = value.astype(F32)
    early, late = target[...].astype(F32), ahead[...].astype(F32)
    rows = eight(
        column_sum(values, values),
        column_sum(values, late),
        column_sum(early, frozen),
        column_sum(late, frozen),
        column_sum(values, frozen),
    )
    fill(sent, value, tail_of(ranks, rows))


def pre_backward(grad, frozen, b_flat, member, sent):
    rank = b_flat.shape[0] // member.shape[0]
    kept = grad[...]
    ranks = select_rank(dot(b_flat[...], kept), member, rank)
    row = column_sum(kept.astype(F32), frozen[...])
    fill(sent, kept, tail_of(ranks, eight(row)))


def pre_plain(grad, b_flat, member, sent):
    rank = b_flat.shape[0] // member.shape[0]
    kept = grad[...]
    ranks = select_rank(dot(b_flat[...], kept), member, rank)
    fill(sent, kept, tail_of(ranks, jnp.zeros((8, kept.shape[1]), F32)))


def row_product(got, weight):
    chips, cols = weight.shape[1], weight.shape[-1]
    total = None
    for j in range(XS):
        part = dot(weight[j].reshape(chips * cols, cols), got[j, :cols])
        total = part if total is None else total + part
    return total.reshape(chips, cols, total.shape[1])


def mid_backward_other(info, got, weight, sent):
    cols = weight.shape[-1]
    main = row_product(got, weight).astype(BF)
    tail = tail_of(*extras(got, cols, got.shape[1] - cols - 16))
    for j in range(sent.shape[0]):
        sent[j, :cols] = main[j]
        sent[j, cols:] = tail


def mid_backward_own(info, got, weight, total):
    total[...] = row_product(got, weight)


def mid_backward(got, total, other, sent):
    cols = total.shape[1]
    rank = got.shape[1] - cols - 16
    ranks, rows = extras(got, cols, rank)
    ranks_o, rows_o = extras(other[:1], cols, rank)
    tail = tail_of(ranks + ranks_o, rows + rows_o)
    for j in range(sent.shape[0]):
        sent[j, :cols] = (total[j] + other[j, :cols].astype(F32)).astype(BF)
        sent[j, cols:] = tail


def add_up(got, total, ranks):
    cols, rank = total.shape[0], ranks.shape[0]
    total[...] = mains(got, cols)
    ranks[...] = extras(got, cols, rank)[0]


def post_target(rank, got, a_turned, member, gain, ahead, store):
    cols = ahead.shape[0]
    ranks, _ = extras(got, cols, rank)
    spread_rank((SCALING * ranks).astype(BF).astype(F32), member, store)
    normed_grad = mains(got, cols) + dot(a_turned[...], store[...])
    ahead[...] = (gain[...] * normed_grad).astype(BF)


def step_back(
    width, grad, back, ranks, row, current, a_turned, member, down_raw, inverse, gain, store
):
    grad_down = (SCALING * ranks).astype(BF).astype(F32)
    spread_rank(grad_down, member, store)
    normed_grad = back + dot(a_turned[...], store[...])
    stat = (row + column_sum(grad_down, down_raw[...])) / width
    scale = inverse[...]
    return (
        grad
        + scale * gain[...] * normed_grad
        - current[...].astype(F32) * (scale * scale * scale * stat)
    ).astype(BF)


def post_backward(
    width, got, grad, current, a_turned, member, down_raw, inverse, gain, grad_in, store
):
    cols, rank = current.shape[0], down_raw.shape[0]
    ranks, rows = extras(got, cols, rank)
    grad_in[...] = step_back(
        width, grad[...].astype(F32), mains(got, cols), ranks, rows[0:1],
        current, a_turned, member, down_raw, inverse, gain, store,
    )


def post_turn(
    width, got, back_first, ranks_first, back_late, ranks_late, target, ahead, result,
    current, a_turned, member, down_raw, inverse, gain, grad, grad_in, store,
):
    cols, rank = current.shape[0], down_raw.shape[0]
    ranks, rows = extras(got, cols, rank)
    scale = lax.rsqrt(rows[0:1] / width + EPSILON)
    least = scale * scale * scale * (rows[1:2] / width)
    fresh = (
        target[...].astype(F32)
        + scale * ahead[...].astype(F32)
        - least * result[...].astype(F32)
    )
    kept = fresh.astype(BF)
    grad[...] = kept
    grad_in[...] = step_back(
        width,
        kept.astype(F32),
        back_first[...] + scale * back_late[...] - least * mains(got, cols),
        ranks_first[...] + scale * ranks_late[...] - least * ranks,
        rows[2:3] + scale * rows[3:4] - least * rows[4:5],
        current, a_turned, member, down_raw, inverse, gain, store,
    )


def ranks_of(flag, received, others, b_flat, member, grad, ranks):
    kept = jnp.where(flag[0] > 0, received[...].astype(F32), others[...].astype(F32)).astype(BF)
    grad[...] = kept
    ranks[...] = select_rank(dot(b_flat[...], kept), member, ranks.shape[0])


def outer_up(down, grad, member, grad_b, store):
    spread_rank(SCALING * down[...].astype(F32), member, store)
    grad_b[...] = dot(store[...], grad[...], ((1,), (1,)))


def outer_down(got, current, inverse, gain, member, grad_a, store):
    ranks = got[0].astype(F32)
    for j in range(1, got.shape[0]):
        ranks = ranks + got[j].astype(F32)
    spread_rank((SCALING * ranks).astype(BF).astype(F32), member, store)
    normed = (current[...].astype(F32) * inverse[...] * gain[...]).astype(BF)
    grad_a[...] = dot(store[...], normed, ((1,), (1,)))


def reorder(weight, block):
    block[0, 0, 0] = weight[0, 0, :, 0]


def cost(flops, arrays):
    return pl.CostEstimate(
        flops=int(flops),
        bytes_accessed=sum(x.size * x.dtype.itemsize for x in arrays),
        transcendentals=0,
    )


def whole_call(body, name, outs, ins, scratch=(), flops=4e8, scalars=0):
    return pl.pallas_call(
        body,
        out_shape=[jax.ShapeDtypeStruct(s, d) for s, d in outs],
        in_specs=[SM] * scalars + [VM] * (len(ins) - scalars),
        out_specs=[VM] * len(outs),
        scratch_shapes=list(scratch),
        compiler_params=PARAMS,
        cost_estimate=cost(flops, ins),
        name=name,
    )(*ins)


def on_device(
    tokens_in, cotangent, base_weight, norm_gain, adapter_a, adapter_b, seg_ids, live_counts
):
    section = lax.axis_index("section")
    at = lax.axis_index("dp")
    at_x, at_y, core = at // (YS * CS), (at // CS) % YS, at % CS
    micro, rows, cols = tokens_in.shape
    total = micro * rows
    adapters, rank = adapter_a.shape[1:3]
    width = base_weight.shape[1]
    tall = cols + rank + 16
    gain = norm_gain[0].astype(F32)[:, None]
    a_flat = adapter_a[0].reshape(adapters * rank, cols)
    b_flat = adapter_b[0].reshape(adapters * rank, cols)
    a_turned, b_turned = a_flat.T, b_flat.T
    member, live = tables_of(seg_ids, live_counts, adapters)
    gain, a_turned, b_turned = lax.optimization_barrier((gain, a_turned, b_turned))
    info = core.astype(jnp.int32).reshape(1)
    store = pltpu.VMEM((adapters * rank, total), BF)
    payload = ((XS, tall, total), BF)
    main = ((cols, total), BF)
    wide = ((cols, total), F32)
    thin = ((rank, total), F32)
    kept_outs = [main, wide, thin, ((1, total), F32), ((rank, total), BF)]

    pair = CS * cols
    block = pl.pallas_call(
        reorder,
        grid=(2, 2, 2),
        in_specs=[
            pl.BlockSpec((1, 1, 2, 1, pair, cols), lambda p, q, i: (i, p, 0, q, 0, 0)),
        ],
        out_specs=pl.BlockSpec((1, 1, 1, 2, pair, cols), lambda p, q, i: (p, q, i, 0, 0, 0)),
        out_shape=jax.ShapeDtypeStruct((2, 2, 2, 2, pair, cols), BF),
        compiler_params=PARAMS,
        name="reorder",
    )(base_weight[0].reshape(2, 2, 2, 2, pair, cols))
    block = exchange(block.reshape(XS, width // XS, cols), BLOCKS)
    halves = block.reshape(XS, YS, CS, cols, cols)
    tokens = tokens_in.reshape(total, cols).T
    target = jnp.where(live[None, :], cotangent.reshape(total, cols).T, jnp.zeros((), BF))

    def mid_call(body, name, steps, specs, ins, out, out_rows, flops, scratch=()):
        return pl.pallas_call(
            body,
            grid_spec=pltpu.PrefetchScalarGridSpec(
                num_scalar_prefetch=1,
                grid=(steps,),
                in_specs=specs,
                out_specs=pl.BlockSpec((XS // steps,) + out_rows, lambda i, c: (i, 0, 0)),
                scratch_shapes=list(scratch),
            ),
            out_shape=jax.ShapeDtypeStruct((XS,) + out_rows, out),
            compiler_params=PARAMS,
            cost_estimate=cost(flops, ins),
            name=name,
        )(info, *ins)

    tall_full = pl.BlockSpec((XS, tall, total), lambda i, c: (0, 0, 0))

    def start_forward(current, out=payload):
        (sent,) = whole_call(pre_forward, "pre_forward", [out], [current, gain, a_flat, member])
        return sent

    def product_forward(got):
        shape = (2, YS, 1, cols, cols)
        other = swap_cores(got)
        own = mid_call(
            mid_forward_own,
            "mid_forward_own",
            2,
            [tall_full, pl.BlockSpec(shape, lambda i, c: (i, 0, c[0], 0, 0))],
            [got, halves],
            F32,
            (total, cols),
            8e8,
            [pltpu.VMEM((total, YS * cols), BF)],
        )
        return mid_call(
            mid_forward,
            "mid_forward",
            2,
            [
                tall_full,
                tall_full,
                pl.BlockSpec(shape, lambda i, c: (i, 0, 1 - c[0], 0, 0)),
                pl.BlockSpec((2, total, cols), lambda i, c: (i, 0, 0)),
            ],
            [got, other, halves, own],
            BF,
            (tall, total),
            8e8,
            [pltpu.VMEM((total, YS * cols), BF)],
        )

    def end_forward(got, current):
        return whole_call(
            functools.partial(post_forward, width),
            "post_forward",
            kept_outs,
            [got, current, b_turned, member],
            scratch=[store],
        )

    def forward(current):
        got = exchange(start_forward(current), APART)
        return exchange(product_forward(got), BLOCKS)

    def product_backward(got):
        shape = (XS, 2, 1, cols, cols)
        other = mid_call(
            mid_backward_other,
            "mid_backward_other",
            2,
            [tall_full, pl.BlockSpec(shape, lambda i, c: (0, i, 1 - c[0], 0, 0))],
            [got, halves],
            BF,
            (tall, total),
            8e8,
        )
        own = mid_call(
            mid_backward_own,
            "mid_backward_own",
            2,
            [tall_full, pl.BlockSpec(shape, lambda i, c: (0, i, c[0], 0, 0))],
            [got, halves],
            F32,
            (cols, total),
            8e8,
        )
        (sent,) = whole_call(
            mid_backward, "mid_backward", [payload], [got, own, swap_cores(other)], flops=1e6
        )
        return sent

    def backward(got):
        return exchange(product_backward(got), APART)

    def plain(vector, out=payload):
        return whole_call(pre_plain, "pre_plain", [out], [vector, b_flat, member])[0]

    def sums_of(got):
        return whole_call(add_up, "add_up", [wide, thin], [backward(got)])

    def zeros(*kinds):
        return [jnp.zeros(*kind) for kind in kinds]

    def hop(value, pairs):
        return lax.ppermute(value, "section", pairs)

    def only(place, work, outs):
        return lax.cond(section == place, lambda: tuple(work()), lambda: tuple(zeros(*outs)))

    single = ((1, tall, total), BF)
    gather = section < 2
    first = jnp.where(gather, start_forward(tokens, single), plain(target, single))
    turns = [first]
    for k in range(1, 4):
        pairs = []
        for i in range(4 * XS * YS * CS):
            s, x, y, c = i // (XS * YS * CS), i // (YS * CS) % XS, i // CS % YS, i % CS
            to = (x ^ (k & 2), y ^ (k & 1) * 2) if s < 2 else partner(x, y, c, k)
            pairs.append((i, s * XS * YS * CS + place(*to, c)))
        turns.append(lax.ppermute(first, ("section", "dp"), pairs))
    turns = jnp.concatenate(turns)
    own = jnp.where(gather, at_x // 2 * 2 + at_y // 2, at_x % 2 * 2 + at_y % 2)
    got = jnp.stack([lax.dynamic_index_in_dim(turns, own ^ j, 0, False) for j in range(4)])

    def run_first():
        outs = end_forward(exchange(product_forward(got), BLOCKS), tokens)
        return outs[0], outs[3], outs[4]

    def run_target():
        return whole_call(
            functools.partial(post_target, rank),
            "post_target",
            [main],
            [backward(got), a_turned, member, gain],
            scratch=[store],
        )

    brief = [main] + kept_outs[3:]
    result_0, inverse_0, down_0 = only(0, run_first, brief)
    first = hop(result_0, [(0, 1)])
    (ahead,) = only(3, run_target, [main])
    ahead = hop(ahead, [(3, 2)])
    back_first, ranks_first = only(2, lambda: sums_of(got), [wide, thin])

    back_late, ranks_late = only(2, lambda: sums_of(exchange(plain(ahead), BLOCKS)), [wide, thin])
    result_1, frozen_1, raw_1, inverse_1, down_1 = only(
        1, lambda: end_forward(forward(first), first), kept_outs
    )
    second = hop(result_1, [(1, 2)])

    def run_turn():
        result, _, raw, inverse, down, sent = whole_call(
            functools.partial(post_forward_turn, width),
            "post_forward_turn",
            kept_outs + [payload],
            [target, ahead, b_flat, forward(second), second, b_turned, member],
            scratch=[store],
        )
        grad, grad_in = whole_call(
            functools.partial(post_turn, width),
            "post_turn",
            [main, main],
            [backward(exchange(sent, BLOCKS)), back_first, ranks_first, back_late, ranks_late, target, ahead]
            + [result, second, a_turned, member, raw, inverse, gain],
            scratch=[store],
        )
        return result, inverse, down, grad, grad_in

    result_2, inverse_2, down_2, grad_2, grad_in = only(2, run_turn, brief + [main, main])
    grad_1 = hop(grad_in, [(2, 1)])
    grad_1, result_2 = lax.optimization_barrier((grad_1, result_2))
    third = hop(result_2, [(2, 3)])

    def run_back():
        (sent,) = whole_call(
            pre_backward, "pre_backward", [payload], [grad_1, frozen_1, b_flat, member]
        )
        return whole_call(
            functools.partial(post_backward, width),
            "post_backward",
            [main],
            [backward(exchange(sent, BLOCKS)), grad_1, first, a_turned, member, raw_1, inverse_1]
            + [gain],
            scratch=[store],
        )

    def run_last():
        outs = end_forward(forward(third), third)
        return outs[0], outs[3], outs[4]

    (grad_in,) = only(1, run_back, [main])
    grad_0 = hop(grad_in, [(1, 0)])
    result_3, inverse_3, down_3 = only(3, run_last, brief)

    def choose(*values):
        return lax.select_n(section.astype(jnp.int32), *values)

    others = choose(target, grad_1, grad_2, target)
    grad, ranks = whole_call(
        ranks_of,
        "ranks_of",
        [main, thin],
        [(section == 0).astype(jnp.int32).reshape(1), grad_0, others, b_flat, member],
        scalars=1,
    )
    ranks = (ranks + swap_cores(ranks)).astype(BF)
    ranks = jnp.broadcast_to(ranks[None], (XS * YS,) + ranks.shape)
    saved = [
        [tokens, first, second, third],
        [result_0, result_1, result_2, result_3],
        [inverse_0, inverse_1, inverse_2, inverse_3],
        [down_0, down_1, down_2, down_3],
    ]
    ranks, saved = lax.optimization_barrier((ranks, saved))
    ranks = exchange(ranks, ALONG_XY)
    current, result, inverse, down = [choose(*values) for values in saved]
    (grad_b,) = whole_call(
        outer_up,
        "outer_up",
        [((adapters * rank, cols), F32)],
        [down, grad, member],
        scratch=[store],
    )
    (grad_a,) = whole_call(
        outer_down,
        "outer_down",
        [((adapters * rank, cols), F32)],
        [ranks, current, inverse, gain, member],
        scratch=[store],
    )
    section_out = result.T.reshape(1, micro, rows, cols)
    shape = (1, adapters, rank, cols)
    return section_out, grad_a.reshape(shape), grad_b.reshape(shape)


def solution(mesh):
    in_specs = (
        P(None, None, "dp"),
        P(None, None, "dp"),
        P("section", None, "dp"),
        P("section", "dp"),
        P("section", None, None, "dp"),
        P("section", None, None, "dp"),
        P(),
        P(),
    )
    out_specs = (
        P("section", None, None, "dp"),
        P("section", None, None, "dp"),
        P("section", None, None, "dp"),
    )
    return jax.shard_map(
        on_device, mesh=mesh, in_specs=in_specs, out_specs=out_specs, check_vma=False
    )
```

```python
import functools

import jax
import jax.numpy as jnp
from jax import lax
from jax.experimental import pallas as pl
from jax.experimental.pallas import tpu as pltpu
from jax.sharding import PartitionSpec as P

EPSILON = 1e-06
SCALING = 2.0
XS, YS, CS = 4, 4, 2
BF = jnp.bfloat16
F32 = jnp.float32
VM = pl.BlockSpec(memory_space=pltpu.VMEM)
SM = pl.BlockSpec(memory_space=pltpu.SMEM)
PARAMS = pltpu.CompilerParams(vmem_limit_bytes=24 << 20)


def place(x, y, c):
    return (x * YS + y) * CS + c


def partner(x, y, c, k):
    other = lambda v: (v ^ 1) if c == 0 else ((v + 1) % 4 if v % 2 else (v - 1) % 4)
    return (other(x) if k & 2 else x), (other(y) if k & 1 else y)


APART = [
    [place(x + 2 * i, y + 2 * j, c) for i in range(2) for j in range(2)]
    for x in range(2)
    for y in range(2)
    for c in range(CS)
]
BLOCKS = [
    [place(*partner(x, y, c, k), c) for k in range(4)]
    for x in range(0, XS, 2)
    for y in range(0, YS, 2)
    for c in range(CS)
]
ALONG_XY = [[place(x, y, c) for x in range(XS) for y in range(YS)] for c in range(CS)]
SIBLING = [(i, i ^ 1) for i in range(XS * YS * CS)]


def exchange(chunks, groups):
    return lax.all_to_all(chunks, "dp", 0, 0, axis_index_groups=groups)


def swap_cores(block):
    return lax.ppermute(block, "dp", SIBLING)


def tables_of(seg_ids, live_counts, adapters):
    micro, rows = seg_ids.shape
    labels = jnp.arange(adapters, dtype=jnp.int32)
    member = (seg_ids[:, None, :] == labels[None, :, None]).astype(jnp.int32)
    counts = jnp.sum(member, axis=2)
    before = (labels[:, None] < labels[None, :]).astype(jnp.int32)
    starts = jnp.sum(counts[:, :, None] * before[None], axis=1)
    row_start = jnp.sum(member * starts[:, :, None], axis=1)
    row_limit = jnp.sum(member * jnp.minimum(live_counts, counts)[:, :, None], axis=1)
    live = jnp.arange(rows, dtype=jnp.int32)[None] - row_start < row_limit
    whole = member.astype(F32).transpose(1, 0, 2).reshape(adapters, micro * rows)
    return whole, live.reshape(micro * rows)


def dot(left, right, dims=((1,), (0,))):
    return lax.dot_general(left, right, (dims, ((), ())), preferred_element_type=F32)


def tail_of(ranks, rows):
    high = rows.astype(BF).astype(F32)
    return jnp.concatenate([ranks, high, rows - high], axis=0).astype(BF)


def eight(*rows):
    index = lax.broadcasted_iota(jnp.int32, (8, rows[0].shape[1]), 0)
    total = jnp.zeros(index.shape, F32)
    for at, row in enumerate(rows):
        total = jnp.where(index == at, row, total)
    return total


def extras(chunks, cols, rank):
    total = chunks[0, cols:].astype(F32)
    for j in range(1, chunks.shape[0]):
        total = total + chunks[j, cols:].astype(F32)
    return total[:rank], total[rank : rank + 8] + total[rank + 8 :]


def mains(chunks, cols):
    total = chunks[0, :cols].astype(F32)
    for j in range(1, chunks.shape[0]):
        total = total + chunks[j, :cols].astype(F32)
    return total


def select_rank(parts, member, rank):
    total = None
    for a in range(member.shape[0]):
        part = parts[a * rank : (a + 1) * rank] * member[a : a + 1, :]
        total = part if total is None else total + part
    return total


def spread_rank(values, member, store):
    rank = values.shape[0]
    for a in range(member.shape[0]):
        store[a * rank : (a + 1) * rank] = (values * member[a : a + 1, :]).astype(BF)


def fill(sent, main, tail):
    cols = main.shape[0]
    for j in range(sent.shape[0]):
        sent[j, :cols] = main
        sent[j, cols:] = tail


def column_sum(left, right):
    return jnp.sum(left * right, axis=0, keepdims=True)


def pre_forward(current, gain, a_flat, member, sent):
    rank = a_flat.shape[0] // member.shape[0]
    values = current[...].astype(F32)
    scaled = (values * gain[...]).astype(BF)
    ranks = select_rank(dot(a_flat[...], scaled), member, rank)
    fill(sent, scaled, tail_of(ranks, eight(column_sum(values, values))))


def turn_rows(got, cols, turned):
    @pl.when(pl.program_id(0) == 0)
    def _():
        turned[...] = got[:, :cols].reshape(got.shape[0] * cols, got.shape[2]).T


def mid_forward_own(info, got, weight, total, turned):
    cols = weight.shape[-1]
    turn_rows(got, cols, turned)
    for i in range(total.shape[0]):
        total[i] = dot(turned[...], weight[i].reshape(YS * cols, cols))


def mid_forward(info, got, other, weight, total, sent, turned):
    cols = weight.shape[-1]
    rank = got.shape[1] - cols - 16
    turn_rows(other, cols, turned)
    ranks, rows = extras(got, cols, rank)
    ranks_o, rows_o = extras(other, cols, rank)
    tail = tail_of(ranks + ranks_o, rows + rows_o)
    for i in range(sent.shape[0]):
        both = total[i] + dot(turned[...], weight[i].reshape(YS * cols, cols))
        sent[i, :cols] = both.astype(BF).T
        sent[i, cols:] = tail


def finish(width, got, current, b_turned, member, result, frozen, down_raw, inverse, down, store):
    cols, rank = current.shape[0], down.shape[0]
    total = mains(got, cols)
    ranks, rows = extras(got, cols, rank)
    scale = lax.rsqrt(rows[0:1] / width + EPSILON)
    kept = (ranks * scale).astype(BF)
    spread_rank(kept.astype(F32), member, store)
    adapter = dot(b_turned[...], store[...])
    value = (current[...].astype(F32) + total * scale + SCALING * adapter).astype(BF)
    result[...] = value
    frozen[...] = total
    down_raw[...] = ranks
    inverse[...] = scale
    down[...] = kept
    return value, total


def post_forward(width, *refs):
    finish(width, *refs)


def post_forward_turn(width, target, ahead, b_flat, *refs):
    sent = refs[-2]
    member, rank = refs[3], refs[-3].shape[0]
    value, frozen = finish(width, *refs[:-2], refs[-1])
    ranks = select_rank(dot(b_flat[...], value), member, rank)
    values = value.astype(F32)
    early, late = target[...].astype(F32), ahead[...].astype(F32)
    rows = eight(
        column_sum(values, values),
        column_sum(values, late),
        column_sum(early, frozen),
        column_sum(late, frozen),
        column_sum(values, frozen),
    )
    fill(sent, value, tail_of(ranks, rows))


def pre_backward(grad, frozen, b_flat, member, sent):
    rank = b_flat.shape[0] // member.shape[0]
    kept = grad[...]
    ranks = select_rank(dot(b_flat[...], kept), member, rank)
    row = column_sum(kept.astype(F32), frozen[...])
    fill(sent, kept, tail_of(ranks, eight(row)))


def pre_plain(grad, b_flat, member, sent):
    rank = b_flat.shape[0] // member.shape[0]
    kept = grad[...]
    ranks = select_rank(dot(b_flat[...], kept), member, rank)
    fill(sent, kept, tail_of(ranks, jnp.zeros((8, kept.shape[1]), F32)))


def row_product(got, weight):
    chips, cols = weight.shape[1], weight.shape[-1]
    left = [weight[j].reshape(chips * cols, cols) for j in range(XS)]
    right = [got[j, :cols] for j in range(XS)]
    total = dot(jnp.concatenate(left, axis=1), jnp.concatenate(right, axis=0))
    return total.reshape(chips, cols, total.shape[1])


def mid_backward_other(info, got, weight, sent):
    cols = weight.shape[-1]
    main = row_product(got, weight).astype(BF)
    tail = tail_of(*extras(got, cols, got.shape[1] - cols - 16))
    for j in range(sent.shape[0]):
        sent[j, :cols] = main[j]
        sent[j, cols:] = tail


def mid_backward_own(info, got, weight, total):
    total[...] = row_product(got, weight)


def mid_backward(got, total, other, sent):
    cols = total.shape[1]
    rank = got.shape[1] - cols - 16
    ranks, rows = extras(got, cols, rank)
    ranks_o, rows_o = extras(other[:1], cols, rank)
    tail = tail_of(ranks + ranks_o, rows + rows_o)
    for j in range(sent.shape[0]):
        sent[j, :cols] = (total[j] + other[j, :cols].astype(F32)).astype(BF)
        sent[j, cols:] = tail


def add_up(got, total, ranks):
    cols, rank = total.shape[0], ranks.shape[0]
    total[...] = mains(got, cols)
    ranks[...] = extras(got, cols, rank)[0]


def post_target(rank, got, a_turned, member, gain, ahead, store):
    cols = ahead.shape[0]
    ranks, _ = extras(got, cols, rank)
    spread_rank((SCALING * ranks).astype(BF).astype(F32), member, store)
    normed_grad = mains(got, cols) + dot(a_turned[...], store[...])
    ahead[...] = (gain[...] * normed_grad).astype(BF)


def step_back(
    width, grad, back, ranks, row, current, a_turned, member, down_raw, inverse, gain, store
):
    grad_down = (SCALING * ranks).astype(BF).astype(F32)
    spread_rank(grad_down, member, store)
    normed_grad = back + dot(a_turned[...], store[...])
    stat = (row + column_sum(grad_down, down_raw[...])) / width
    scale = inverse[...]
    return (
        grad
        + scale * gain[...] * normed_grad
        - current[...].astype(F32) * (scale * scale * scale * stat)
    ).astype(BF)


def post_backward(
    width, got, grad, current, a_turned, member, down_raw, inverse, gain, grad_in, store
):
    cols, rank = current.shape[0], down_raw.shape[0]
    ranks, rows = extras(got, cols, rank)
    grad_in[...] = step_back(
        width, grad[...].astype(F32), mains(got, cols), ranks, rows[0:1],
        current, a_turned, member, down_raw, inverse, gain, store,
    )


def post_turn(
    width, got, back_first, ranks_first, back_late, ranks_late, target, ahead, result,
    current, a_turned, member, down_raw, inverse, gain, grad, grad_in, store,
):
    cols, rank = current.shape[0], down_raw.shape[0]
    ranks, rows = extras(got, cols, rank)
    scale = lax.rsqrt(rows[0:1] / width + EPSILON)
    least = scale * scale * scale * (rows[1:2] / width)
    fresh = (
        target[...].astype(F32)
        + scale * ahead[...].astype(F32)
        - least * result[...].astype(F32)
    )
    kept = fresh.astype(BF)
    grad[...] = kept
    grad_in[...] = step_back(
        width,
        kept.astype(F32),
        back_first[...] + scale * back_late[...] - least * mains(got, cols),
        ranks_first[...] + scale * ranks_late[...] - least * ranks,
        rows[2:3] + scale * rows[3:4] - least * rows[4:5],
        current, a_turned, member, down_raw, inverse, gain, store,
    )


def ranks_of(flag, received, others, b_flat, member, grad, ranks):
    kept = jnp.where(flag[0] > 0, received[...].astype(F32), others[...].astype(F32)).astype(BF)
    grad[...] = kept
    ranks[...] = select_rank(dot(b_flat[...], kept), member, ranks.shape[0])


def both_cores(ranks, other, sent):
    both = (ranks[...] + other[...]).astype(BF)
    for j in range(sent.shape[0]):
        sent[j] = both


def outer_up(down, grad, member, grad_b, store):
    spread_rank(SCALING * down[...].astype(F32), member, store)
    grad_b[...] = dot(store[...], grad[...], ((1,), (1,)))


def outer_down(got, current, inverse, gain, member, grad_a, store):
    ranks = got[0].astype(F32)
    for j in range(1, got.shape[0]):
        ranks = ranks + got[j].astype(F32)
    spread_rank((SCALING * ranks).astype(BF).astype(F32), member, store)
    normed = (current[...].astype(F32) * inverse[...] * gain[...]).astype(BF)
    grad_a[...] = dot(store[...], normed, ((1,), (1,)))


def reorder(weight, block):
    block[0, 0, 0] = weight[0, 0, :, 0]


def bring(block, kept, sem):
    copy = pltpu.make_async_copy(block, kept, sem)
    copy.start()
    copy.wait()


def cost(flops, arrays):
    return pl.CostEstimate(
        flops=int(flops),
        bytes_accessed=sum(x.size * x.dtype.itemsize for x in arrays),
        transcendentals=0,
    )


def held(value):
    return pltpu.with_memory_space_constraint(value, pltpu.VMEM)


def whole_call(body, name, outs, ins, scratch=(), flops=4e8, scalars=0):
    return pl.pallas_call(
        body,
        out_shape=[jax.ShapeDtypeStruct(s, d) for s, d in outs],
        in_specs=[SM] * scalars + [VM] * (len(ins) - scalars),
        out_specs=[VM] * len(outs),
        scratch_shapes=list(scratch),
        compiler_params=PARAMS,
        cost_estimate=cost(flops, ins),
        name=name,
    )(*ins)


def on_device(
    tokens_in, cotangent, base_weight, norm_gain, adapter_a, adapter_b, seg_ids, live_counts
):
    section = lax.axis_index("section")
    at = lax.axis_index("dp")
    at_x, at_y, core = at // (YS * CS), (at // CS) % YS, at % CS
    micro, rows, cols = tokens_in.shape
    total = micro * rows
    adapters, rank = adapter_a.shape[1:3]
    width = base_weight.shape[1]
    tall = cols + rank + 16
    gain = norm_gain[0].astype(F32)[:, None]
    a_flat = adapter_a[0].reshape(adapters * rank, cols)
    b_flat = adapter_b[0].reshape(adapters * rank, cols)
    a_turned, b_turned = a_flat.T, b_flat.T
    member, live = tables_of(seg_ids, live_counts, adapters)
    gain, a_turned, b_turned = lax.optimization_barrier((gain, a_turned, b_turned))
    info = core.astype(jnp.int32).reshape(1)
    store = pltpu.VMEM((adapters * rank, total), BF)
    payload = ((XS, tall, total), BF)
    main = ((cols, total), BF)
    wide = ((cols, total), F32)
    thin = ((rank, total), F32)
    kept_outs = [main, wide, thin, ((1, total), F32), ((rank, total), BF)]

    pair = CS * cols
    block = pl.pallas_call(
        reorder,
        grid=(2, 2, 2),
        in_specs=[
            pl.BlockSpec((1, 1, 2, 1, pair, cols), lambda p, q, i: (i, p, 0, q, 0, 0)),
        ],
        out_specs=pl.BlockSpec((1, 1, 1, 2, pair, cols), lambda p, q, i: (p, q, i, 0, 0, 0)),
        out_shape=jax.ShapeDtypeStruct((2, 2, 2, 2, pair, cols), BF),
        compiler_params=PARAMS,
        name="reorder",
    )(base_weight[0].reshape(2, 2, 2, 2, pair, cols))
    block = exchange(block.reshape(XS, width // XS, cols), BLOCKS)
    halves = block.reshape(XS, YS, CS, cols, cols)
    tokens = tokens_in.reshape(total, cols).T
    target = jnp.where(live[None, :], cotangent.reshape(total, cols).T, jnp.zeros((), BF))

    def mid_call(body, name, steps, specs, ins, out, out_rows, flops, scratch=()):
        return pl.pallas_call(
            body,
            grid_spec=pltpu.PrefetchScalarGridSpec(
                num_scalar_prefetch=1,
                grid=(steps,),
                in_specs=specs,
                out_specs=pl.BlockSpec((XS // steps,) + out_rows, lambda i, c: (i, 0, 0)),
                scratch_shapes=list(scratch),
            ),
            out_shape=jax.ShapeDtypeStruct((XS,) + out_rows, out),
            compiler_params=PARAMS,
            cost_estimate=cost(flops, ins),
            name=name,
        )(info, *ins)

    tall_full = pl.BlockSpec((XS, tall, total), lambda i, c: (0, 0, 0))

    def start_forward(current, out=payload):
        (sent,) = whole_call(pre_forward, "pre_forward", [out], [current, gain, a_flat, member])
        return sent

    def near(value):
        return pl.pallas_call(
            bring,
            out_shape=pltpu.VMEM(value.shape, value.dtype),
            in_specs=[pl.BlockSpec(memory_space=pl.ANY)],
            out_specs=VM,
            scratch_shapes=[pltpu.SemaphoreType.DMA],
            compiler_params=PARAMS,
            cost_estimate=cost(8e8, [value]),
            name="bring",
        )(value)

    def product_forward(got, held=held):
        shape = (2, YS, 1, cols, cols)
        other = swap_cores(got)
        own = mid_call(
            mid_forward_own,
            "mid_forward_own",
            2,
            [tall_full, pl.BlockSpec(shape, lambda i, c: (i, 0, c[0], 0, 0))],
            [got, held(halves)],
            F32,
            (total, cols),
            8e8,
            [pltpu.VMEM((total, YS * cols), BF)],
        )
        return mid_call(
            mid_forward,
            "mid_forward",
            2,
            [
                tall_full,
                tall_full,
                pl.BlockSpec(shape, lambda i, c: (i, 0, 1 - c[0], 0, 0)),
                pl.BlockSpec((2, total, cols), lambda i, c: (i, 0, 0)),
            ],
            [got, other, held(halves), own],
            BF,
            (tall, total),
            8e8,
            [pltpu.VMEM((total, YS * cols), BF)],
        )

    def end_forward(got, current):
        return whole_call(
            functools.partial(post_forward, width),
            "post_forward",
            kept_outs,
            [got, current, b_turned, member],
            scratch=[store],
        )

    def forward(current):
        got = exchange(start_forward(current), APART)
        return exchange(product_forward(got), BLOCKS)

    def product_backward(got, held=held):
        shape = (XS, 2, 1, cols, cols)
        other = mid_call(
            mid_backward_other,
            "mid_backward_other",
            2,
            [tall_full, pl.BlockSpec(shape, lambda i, c: (0, i, 1 - c[0], 0, 0))],
            [got, held(halves)],
            BF,
            (tall, total),
            8e8,
        )
        own = mid_call(
            mid_backward_own,
            "mid_backward_own",
            2,
            [tall_full, pl.BlockSpec(shape, lambda i, c: (0, i, c[0], 0, 0))],
            [got, held(halves)],
            F32,
            (cols, total),
            8e8,
        )
        (sent,) = whole_call(
            mid_backward, "mid_backward", [payload], [got, own, swap_cores(other)], flops=1e6
        )
        return sent

    def backward(got, held=held):
        return exchange(product_backward(got, held), APART)

    def plain(vector, out=payload):
        return whole_call(pre_plain, "pre_plain", [out], [vector, b_flat, member])[0]

    def sums_of(got):
        return whole_call(add_up, "add_up", [wide, thin], [backward(got, lambda x: x)])

    def zeros(*kinds):
        return [jnp.zeros(*kind) for kind in kinds]

    def hop(value, pairs):
        return lax.ppermute(value, "section", pairs)

    def only(place, work, outs):
        return lax.cond(section == place, lambda: tuple(work()), lambda: tuple(zeros(*outs)))

    single = ((1, tall, total), BF)
    gather = section < 2
    first = jnp.where(gather, start_forward(tokens, single), plain(target, single))
    turns = [first]
    for k in range(1, 4):
        pairs = []
        for i in range(4 * XS * YS * CS):
            s, x, y, c = i // (XS * YS * CS), i // (YS * CS) % XS, i // CS % YS, i % CS
            to = (x ^ (k & 2), y ^ (k & 1) * 2) if s < 2 else partner(x, y, c, k)
            pairs.append((i, s * XS * YS * CS + place(*to, c)))
        turns.append(lax.ppermute(first, ("section", "dp"), pairs))
    turns = jnp.concatenate(turns)
    own = jnp.where(gather, at_x // 2 * 2 + at_y // 2, at_x % 2 * 2 + at_y % 2)
    got = jnp.stack([lax.dynamic_index_in_dim(turns, own ^ j, 0, False) for j in range(4)])

    def run_first():
        outs = end_forward(exchange(product_forward(got, lambda x: x), BLOCKS), tokens)
        return outs[0], outs[3], outs[4]

    def run_target():
        return whole_call(
            functools.partial(post_target, rank),
            "post_target",
            [main],
            [backward(got, lambda x: x), a_turned, member, gain],
            scratch=[store],
        )

    brief = [main] + kept_outs[3:]
    result_0, inverse_0, down_0 = only(0, run_first, brief)
    first = hop(result_0, [(0, 1)])
    (ahead,) = only(3, run_target, [main])
    ahead = hop(ahead, [(3, 2)])
    back_first, ranks_first = only(2, lambda: sums_of(got), [wide, thin])

    back_late, ranks_late = only(2, lambda: sums_of(exchange(plain(ahead), BLOCKS)), [wide, thin])
    halves, back_first = lax.optimization_barrier((halves, back_first))
    halves = near(halves)
    result_1, frozen_1, raw_1, inverse_1, down_1 = only(
        1, lambda: end_forward(forward(first), first), kept_outs
    )
    second = hop(result_1, [(1, 2)])

    def run_turn():
        result, _, raw, inverse, down, sent = whole_call(
            functools.partial(post_forward_turn, width),
            "post_forward_turn",
            kept_outs + [payload],
            [target, ahead, b_flat, forward(second), second, b_turned, member],
            scratch=[store],
        )
        grad, grad_in = whole_call(
            functools.partial(post_turn, width),
            "post_turn",
            [main, main],
            [backward(exchange(sent, BLOCKS)), back_first, ranks_first, back_late, ranks_late, target, ahead]
            + [result, second, a_turned, member, raw, inverse, gain],
            scratch=[store],
        )
        return result, inverse, down, grad, grad_in

    result_2, inverse_2, down_2, grad_2, grad_in = only(2, run_turn, brief + [main, main])
    grad_1 = hop(grad_in, [(2, 1)])
    grad_1, result_2 = lax.optimization_barrier((grad_1, result_2))
    third = hop(result_2, [(2, 3)])

    def run_back():
        (sent,) = whole_call(
            pre_backward, "pre_backward", [payload], [grad_1, frozen_1, b_flat, member]
        )
        return whole_call(
            functools.partial(post_backward, width),
            "post_backward",
            [main],
            [backward(exchange(sent, BLOCKS)), grad_1, first, a_turned, member, raw_1, inverse_1]
            + [gain],
            scratch=[store],
        )

    def run_last():
        outs = end_forward(forward(third), third)
        return outs[0], outs[3], outs[4]

    (grad_in,) = only(1, run_back, [main])
    grad_0 = hop(grad_in, [(1, 0)])
    result_3, inverse_3, down_3 = only(3, run_last, brief)

    def choose(*values):
        return lax.select_n(section.astype(jnp.int32), *values)

    others = choose(target, grad_1, grad_2, target)
    others, result_3 = lax.optimization_barrier((others, result_3))
    grad, ranks = whole_call(
        ranks_of,
        "ranks_of",
        [main, thin],
        [(section == 0).astype(jnp.int32).reshape(1), grad_0, others, b_flat, member],
        scalars=1,
    )
    (ranks,) = whole_call(
        both_cores,
        "both_cores",
        [((XS * YS, rank, total), BF)],
        [ranks, swap_cores(ranks)],
        flops=1e6,
    )
    saved = [
        [tokens, first, second, third],
        [result_0, result_1, result_2, result_3],
        [inverse_0, inverse_1, inverse_2, inverse_3],
        [down_0, down_1, down_2, down_3],
    ]
    ranks, saved = lax.optimization_barrier((ranks, saved))
    ranks = exchange(ranks, ALONG_XY)
    current, result, inverse, down = [choose(*values) for values in saved]
    (grad_b,) = whole_call(
        outer_up,
        "outer_up",
        [((adapters * rank, cols), F32)],
        [down, grad, member],
        scratch=[store],
    )
    (grad_a,) = whole_call(
        outer_down,
        "outer_down",
        [((adapters * rank, cols), F32)],
        [ranks, current, inverse, gain, member],
        scratch=[store],
    )
    section_out = result.T.reshape(1, micro, rows, cols)
    shape = (1, adapters, rank, cols)
    return section_out, grad_a.reshape(shape), grad_b.reshape(shape)


def solution(mesh):
    in_specs = (
        P(None, None, "dp"),
        P(None, None, "dp"),
        P("section", None, "dp"),
        P("section", "dp"),
        P("section", None, None, "dp"),
        P("section", None, None, "dp"),
        P(),
        P(),
    )
    out_specs = (
        P("section", None, None, "dp"),
        P("section", None, None, "dp"),
        P("section", None, None, "dp"),
    )
    return jax.shard_map(
        on_device, mesh=mesh, in_specs=in_specs, out_specs=out_specs, check_vma=False
    )
```

```python
import functools

import jax
import jax.numpy as jnp
from jax import lax
from jax.experimental import pallas as pl
from jax.experimental.pallas import tpu as pltpu
from jax.sharding import PartitionSpec as P

EPSILON = 1e-06
SCALING = 2.0
XS, YS, CS = 4, 4, 2
BF = jnp.bfloat16
F32 = jnp.float32
VM = pl.BlockSpec(memory_space=pltpu.VMEM)
SM = pl.BlockSpec(memory_space=pltpu.SMEM)
PARAMS = pltpu.CompilerParams(vmem_limit_bytes=24 << 20)


def place(x, y, c):
    return (x * YS + y) * CS + c


def partner(x, y, c, k):
    other = lambda v: (v ^ 1) if c == 0 else ((v + 1) % 4 if v % 2 else (v - 1) % 4)
    return (other(x) if k & 2 else x), (other(y) if k & 1 else y)


APART = [
    [place(x + 2 * i, y + 2 * j, c) for i in range(2) for j in range(2)]
    for x in range(2)
    for y in range(2)
    for c in range(CS)
]
ROUND = (0, 1, 3, 2)
RING = [[group[k] for k in ROUND] for group in APART]
BLOCKS = [
    [place(*partner(x, y, c, k), c) for k in range(4)]
    for x in range(0, XS, 2)
    for y in range(0, YS, 2)
    for c in range(CS)
]
ALONG_XY = [[place(x, y, c) for x in range(XS) for y in range(YS)] for c in range(CS)]
SIBLING = [(i, i ^ 1) for i in range(XS * YS * CS)]


def exchange(chunks, groups):
    return lax.all_to_all(chunks, "dp", 0, 0, axis_index_groups=groups)


def swap_cores(block):
    return lax.ppermute(block, "dp", SIBLING)


def tables_of(seg_ids, live_counts, adapters):
    micro, rows = seg_ids.shape
    labels = jnp.arange(adapters, dtype=jnp.int32)
    member = (seg_ids[:, None, :] == labels[None, :, None]).astype(jnp.int32)
    counts = jnp.sum(member, axis=2)
    before = (labels[:, None] < labels[None, :]).astype(jnp.int32)
    starts = jnp.sum(counts[:, :, None] * before[None], axis=1)
    row_start = jnp.sum(member * starts[:, :, None], axis=1)
    row_limit = jnp.sum(member * jnp.minimum(live_counts, counts)[:, :, None], axis=1)
    live = jnp.arange(rows, dtype=jnp.int32)[None] - row_start < row_limit
    whole = member.astype(F32).transpose(1, 0, 2).reshape(adapters, micro * rows)
    return whole, live.reshape(micro * rows)


def dot(left, right, dims=((1,), (0,))):
    return lax.dot_general(left, right, (dims, ((), ())), preferred_element_type=F32)


def tail_of(ranks, rows):
    high = rows.astype(BF).astype(F32)
    return jnp.concatenate([ranks, high, rows - high], axis=0).astype(BF)


def eight(*rows):
    index = lax.broadcasted_iota(jnp.int32, (8, rows[0].shape[1]), 0)
    total = jnp.zeros(index.shape, F32)
    for at, row in enumerate(rows):
        total = jnp.where(index == at, row, total)
    return total


def extras(chunks, cols, rank):
    total = chunks[0, cols:].astype(F32)
    for j in range(1, chunks.shape[0]):
        total = total + chunks[j, cols:].astype(F32)
    return total[:rank], total[rank : rank + 8] + total[rank + 8 :]


def mains(chunks, cols):
    total = chunks[0, :cols].astype(F32)
    for j in range(1, chunks.shape[0]):
        total = total + chunks[j, :cols].astype(F32)
    return total


def select_rank(parts, member, rank):
    total = None
    for a in range(member.shape[0]):
        part = parts[a * rank : (a + 1) * rank] * member[a : a + 1, :]
        total = part if total is None else total + part
    return total


def spread_rank(values, member, store):
    rank = values.shape[0]
    for a in range(member.shape[0]):
        store[a * rank : (a + 1) * rank] = (values * member[a : a + 1, :]).astype(BF)


def fill(sent, main, tail):
    cols = main.shape[0]
    for j in range(sent.shape[0]):
        sent[j, :cols] = main
        sent[j, cols:] = tail


def column_sum(left, right):
    return jnp.sum(left * right, axis=0, keepdims=True)


def pre_forward(current, gain, a_flat, member, sent):
    rank = a_flat.shape[0] // member.shape[0]
    values = current[...].astype(F32)
    scaled = (values * gain[...]).astype(BF)
    ranks = select_rank(dot(a_flat[...], scaled), member, rank)
    fill(sent, scaled, tail_of(ranks, eight(column_sum(values, values))))


def turn_rows(got, cols, turned):
    @pl.when(pl.program_id(0) == 0)
    def _():
        parts = [got[k, :cols] for k in ROUND]
        turned[...] = jnp.concatenate(parts, axis=0).T


def mid_forward_own(info, got, weight, total, turned):
    cols = weight.shape[-1]
    turn_rows(got, cols, turned)
    for i in range(total.shape[0]):
        total[i] = dot(turned[...], weight[i].reshape(YS * cols, cols))


def mid_forward(info, got, other, weight, total, sent, turned):
    cols = weight.shape[-1]
    rank = got.shape[1] - cols - 16
    turn_rows(other, cols, turned)
    ranks, rows = extras(got, cols, rank)
    ranks_o, rows_o = extras(other, cols, rank)
    tail = tail_of(ranks + ranks_o, rows + rows_o)
    for i in range(sent.shape[0]):
        both = total[i] + dot(turned[...], weight[i].reshape(YS * cols, cols))
        sent[i, :cols] = both.astype(BF).T
        sent[i, cols:] = tail


def finish(width, got, current, b_turned, member, result, frozen, down_raw, inverse, down, store):
    cols, rank = current.shape[0], down.shape[0]
    total = mains(got, cols)
    ranks, rows = extras(got, cols, rank)
    scale = lax.rsqrt(rows[0:1] / width + EPSILON)
    kept = (ranks * scale).astype(BF)
    spread_rank(kept.astype(F32), member, store)
    adapter = dot(b_turned[...], store[...])
    value = (current[...].astype(F32) + total * scale + SCALING * adapter).astype(BF)
    result[...] = value
    frozen[...] = total
    down_raw[...] = ranks
    inverse[...] = scale
    down[...] = kept
    return value, total


def post_forward(width, *refs):
    finish(width, *refs)


def post_forward_turn(width, target, ahead, b_flat, *refs):
    sent = refs[-2]
    member, rank = refs[3], refs[-3].shape[0]
    value, frozen = finish(width, *refs[:-2], refs[-1])
    ranks = select_rank(dot(b_flat[...], value), member, rank)
    values = value.astype(F32)
    early, late = target[...].astype(F32), ahead[...].astype(F32)
    rows = eight(
        column_sum(values, values),
        column_sum(values, late),
        column_sum(early, frozen),
        column_sum(late, frozen),
        column_sum(values, frozen),
    )
    fill(sent, value, tail_of(ranks, rows))


def pre_backward(grad, frozen, b_flat, member, sent):
    rank = b_flat.shape[0] // member.shape[0]
    kept = grad[...]
    ranks = select_rank(dot(b_flat[...], kept), member, rank)
    row = column_sum(kept.astype(F32), frozen[...])
    fill(sent, kept, tail_of(ranks, eight(row)))


def pre_plain(grad, b_flat, member, sent):
    rank = b_flat.shape[0] // member.shape[0]
    kept = grad[...]
    ranks = select_rank(dot(b_flat[...], kept), member, rank)
    fill(sent, kept, tail_of(ranks, jnp.zeros((8, kept.shape[1]), F32)))


def row_product(got, weight):
    chips, cols = weight.shape[1], weight.shape[-1]
    left = [weight[j].reshape(chips * cols, cols) for j in range(XS)]
    right = [got[j, :cols] for j in range(XS)]
    total = dot(jnp.concatenate(left, axis=1), jnp.concatenate(right, axis=0))
    return total.reshape(chips, cols, total.shape[1])


def mid_backward_other(info, got, weight, sent):
    cols = weight.shape[-1]
    main = row_product(got, weight).astype(BF)
    tail = tail_of(*extras(got, cols, got.shape[1] - cols - 16))
    for j in range(sent.shape[0]):
        sent[j, :cols] = main[j]
        sent[j, cols:] = tail


def mid_backward_own(info, got, weight, total):
    total[...] = row_product(got, weight)


def mid_backward(got, total, other, sent):
    cols = total.shape[1]
    rank = got.shape[1] - cols - 16
    ranks, rows = extras(got, cols, rank)
    ranks_o, rows_o = extras(other[:1], cols, rank)
    tail = tail_of(ranks + ranks_o, rows + rows_o)
    for j in range(sent.shape[0]):
        sent[j, :cols] = (total[j] + other[j, :cols].astype(F32)).astype(BF)
        sent[j, cols:] = tail


def add_up(got, total, ranks):
    cols, rank = total.shape[0], ranks.shape[0]
    total[...] = mains(got, cols)
    ranks[...] = extras(got, cols, rank)[0]


def post_target(rank, got, a_turned, member, gain, ahead, store):
    cols = ahead.shape[0]
    ranks, _ = extras(got, cols, rank)
    spread_rank((SCALING * ranks).astype(BF).astype(F32), member, store)
    normed_grad = mains(got, cols) + dot(a_turned[...], store[...])
    ahead[...] = (gain[...] * normed_grad).astype(BF)


def step_back(
    width, grad, back, ranks, row, current, a_turned, member, down_raw, inverse, gain, store
):
    grad_down = (SCALING * ranks).astype(BF).astype(F32)
    spread_rank(grad_down, member, store)
    normed_grad = back + dot(a_turned[...], store[...])
    stat = (row + column_sum(grad_down, down_raw[...])) / width
    scale = inverse[...]
    return (
        grad
        + scale * gain[...] * normed_grad
        - current[...].astype(F32) * (scale * scale * scale * stat)
    ).astype(BF)


def post_backward(
    width, got, grad, current, a_turned, member, down_raw, inverse, gain, grad_in, store
):
    cols, rank = current.shape[0], down_raw.shape[0]
    ranks, rows = extras(got, cols, rank)
    grad_in[...] = step_back(
        width, grad[...].astype(F32), mains(got, cols), ranks, rows[0:1],
        current, a_turned, member, down_raw, inverse, gain, store,
    )


def post_turn(
    width, got, back_first, ranks_first, back_late, ranks_late, target, ahead, result,
    current, a_turned, member, down_raw, inverse, gain, grad, grad_in, store,
):
    cols, rank = current.shape[0], down_raw.shape[0]
    ranks, rows = extras(got, cols, rank)
    scale = lax.rsqrt(rows[0:1] / width + EPSILON)
    least = scale * scale * scale * (rows[1:2] / width)
    fresh = (
        target[...].astype(F32)
        + scale * ahead[...].astype(F32)
        - least * result[...].astype(F32)
    )
    kept = fresh.astype(BF)
    grad[...] = kept
    grad_in[...] = step_back(
        width,
        kept.astype(F32),
        back_first[...] + scale * back_late[...] - least * mains(got, cols),
        ranks_first[...] + scale * ranks_late[...] - least * ranks,
        rows[2:3] + scale * rows[3:4] - least * rows[4:5],
        current, a_turned, member, down_raw, inverse, gain, store,
    )


def ranks_of(flag, received, others, b_flat, member, grad, ranks):
    kept = jnp.where(flag[0] > 0, received[...].astype(F32), others[...].astype(F32)).astype(BF)
    grad[...] = kept
    ranks[...] = select_rank(dot(b_flat[...], kept), member, ranks.shape[0])


def both_cores(ranks, other, sent):
    both = (ranks[...] + other[...]).astype(BF)
    for j in range(sent.shape[0]):
        sent[j] = both


def outer_up(down, grad, member, grad_b, store):
    spread_rank(SCALING * down[...].astype(F32), member, store)
    grad_b[...] = dot(store[...], grad[...], ((1,), (1,)))


def outer_down(got, current, inverse, gain, member, grad_a, store):
    ranks = got[0].astype(F32)
    for j in range(1, got.shape[0]):
        ranks = ranks + got[j].astype(F32)
    spread_rank((SCALING * ranks).astype(BF).astype(F32), member, store)
    normed = (current[...].astype(F32) * inverse[...] * gain[...]).astype(BF)
    grad_a[...] = dot(store[...], normed, ((1,), (1,)))


def reorder(weight, block):
    block[0, 0, 0] = weight[0, 0, :, 0]


def bring(block, kept, sem):
    copy = pltpu.make_async_copy(block, kept, sem)
    copy.start()
    copy.wait()


def cost(flops, arrays):
    return pl.CostEstimate(
        flops=int(flops),
        bytes_accessed=sum(x.size * x.dtype.itemsize for x in arrays),
        transcendentals=0,
    )


def held(value):
    return pltpu.with_memory_space_constraint(value, pltpu.VMEM)


def whole_call(body, name, outs, ins, scratch=(), flops=4e8, scalars=0):
    return pl.pallas_call(
        body,
        out_shape=[jax.ShapeDtypeStruct(s, d) for s, d in outs],
        in_specs=[SM] * scalars + [VM] * (len(ins) - scalars),
        out_specs=[VM] * len(outs),
        scratch_shapes=list(scratch),
        compiler_params=PARAMS,
        cost_estimate=cost(flops, ins),
        name=name,
    )(*ins)


def on_device(
    tokens_in, cotangent, base_weight, norm_gain, adapter_a, adapter_b, seg_ids, live_counts
):
    section = lax.axis_index("section")
    at = lax.axis_index("dp")
    at_x, at_y, core = at // (YS * CS), (at // CS) % YS, at % CS
    micro, rows, cols = tokens_in.shape
    total = micro * rows
    adapters, rank = adapter_a.shape[1:3]
    width = base_weight.shape[1]
    tall = cols + rank + 16
    gain = norm_gain[0].astype(F32)[:, None]
    a_flat = adapter_a[0].reshape(adapters * rank, cols)
    b_flat = adapter_b[0].reshape(adapters * rank, cols)
    a_turned, b_turned = a_flat.T, b_flat.T
    member, live = tables_of(seg_ids, live_counts, adapters)
    gain, a_turned, b_turned = lax.optimization_barrier((gain, a_turned, b_turned))
    info = core.astype(jnp.int32).reshape(1)
    store = pltpu.VMEM((adapters * rank, total), BF)
    payload = ((XS, tall, total), BF)
    main = ((cols, total), BF)
    wide = ((cols, total), F32)
    thin = ((rank, total), F32)
    kept_outs = [main, wide, thin, ((1, total), F32), ((rank, total), BF)]

    pair = CS * cols
    block = pl.pallas_call(
        reorder,
        grid=(2, 2, 2),
        in_specs=[
            pl.BlockSpec((1, 1, 2, 1, pair, cols), lambda p, q, i: (i, p, 0, q, 0, 0)),
        ],
        out_specs=pl.BlockSpec((1, 1, 1, 2, pair, cols), lambda p, q, i: (p, q, i, 0, 0, 0)),
        out_shape=jax.ShapeDtypeStruct((2, 2, 2, 2, pair, cols), BF),
        compiler_params=PARAMS,
        name="reorder",
    )(base_weight[0].reshape(2, 2, 2, 2, pair, cols))
    block = exchange(block.reshape(XS, width // XS, cols), BLOCKS)
    halves = block.reshape(XS, YS, CS, cols, cols)
    tokens = tokens_in.reshape(total, cols).T
    target = jnp.where(live[None, :], cotangent.reshape(total, cols).T, jnp.zeros((), BF))

    def mid_call(body, name, steps, specs, ins, out, out_rows, flops, scratch=()):
        return pl.pallas_call(
            body,
            grid_spec=pltpu.PrefetchScalarGridSpec(
                num_scalar_prefetch=1,
                grid=(steps,),
                in_specs=specs,
                out_specs=pl.BlockSpec((XS // steps,) + out_rows, lambda i, c: (i, 0, 0)),
                scratch_shapes=list(scratch),
            ),
            out_shape=jax.ShapeDtypeStruct((XS,) + out_rows, out),
            compiler_params=PARAMS,
            cost_estimate=cost(flops, ins),
            name=name,
        )(info, *ins)

    tall_full = pl.BlockSpec((XS, tall, total), lambda i, c: (0, 0, 0))

    def start_forward(current, out=payload):
        (sent,) = whole_call(pre_forward, "pre_forward", [out], [current, gain, a_flat, member])
        return sent

    def near(value):
        return pl.pallas_call(
            bring,
            out_shape=pltpu.VMEM(value.shape, value.dtype),
            in_specs=[pl.BlockSpec(memory_space=pl.ANY)],
            out_specs=VM,
            scratch_shapes=[pltpu.SemaphoreType.DMA],
            compiler_params=PARAMS,
            cost_estimate=cost(8e8, [value]),
            name="bring",
        )(value)

    def product_forward(got, held=held):
        shape = (2, YS, 1, cols, cols)
        other = swap_cores(got)
        own = mid_call(
            mid_forward_own,
            "mid_forward_own",
            2,
            [tall_full, pl.BlockSpec(shape, lambda i, c: (i, 0, c[0], 0, 0))],
            [got, held(halves)],
            F32,
            (total, cols),
            8e8,
            [pltpu.VMEM((total, YS * cols), BF)],
        )
        return mid_call(
            mid_forward,
            "mid_forward",
            2,
            [
                tall_full,
                tall_full,
                pl.BlockSpec(shape, lambda i, c: (i, 0, 1 - c[0], 0, 0)),
                pl.BlockSpec((2, total, cols), lambda i, c: (i, 0, 0)),
            ],
            [got, other, held(halves), own],
            BF,
            (tall, total),
            8e8,
            [pltpu.VMEM((total, YS * cols), BF)],
        )

    def end_forward(got, current):
        return whole_call(
            functools.partial(post_forward, width),
            "post_forward",
            kept_outs,
            [got, current, b_turned, member],
            scratch=[store],
        )

    def forward(current):
        sent = start_forward(current, ((1, tall, total), BF))
        got = lax.all_gather(sent, "dp", axis_index_groups=RING, axis=0, tiled=True)
        return exchange(product_forward(got), BLOCKS)

    def product_backward(got, held=held):
        shape = (XS, 2, 1, cols, cols)
        other = mid_call(
            mid_backward_other,
            "mid_backward_other",
            2,
            [tall_full, pl.BlockSpec(shape, lambda i, c: (0, i, 1 - c[0], 0, 0))],
            [got, held(halves)],
            BF,
            (tall, total),
            8e8,
        )
        own = mid_call(
            mid_backward_own,
            "mid_backward_own",
            2,
            [tall_full, pl.BlockSpec(shape, lambda i, c: (0, i, c[0], 0, 0))],
            [got, held(halves)],
            F32,
            (cols, total),
            8e8,
        )
        (sent,) = whole_call(
            mid_backward, "mid_backward", [payload], [got, own, swap_cores(other)], flops=1e6
        )
        return sent

    def backward(got, held=held):
        return exchange(product_backward(got, held), APART)

    def plain(vector, out=payload):
        return whole_call(pre_plain, "pre_plain", [out], [vector, b_flat, member])[0]

    def sums_of(got):
        return whole_call(add_up, "add_up", [wide, thin], [backward(got, lambda x: x)])

    def zeros(*kinds):
        return [jnp.zeros(*kind) for kind in kinds]

    def hop(value, pairs):
        return lax.ppermute(value, "section", pairs)

    def only(place, work, outs):
        return lax.cond(section == place, lambda: tuple(work()), lambda: tuple(zeros(*outs)))

    single = ((1, tall, total), BF)
    gather = section < 2
    first = jnp.where(gather, start_forward(tokens, single), plain(target, single))
    turns = [first]
    for k in range(1, 4):
        pairs = []
        for i in range(4 * XS * YS * CS):
            s, x, y, c = i // (XS * YS * CS), i // (YS * CS) % XS, i // CS % YS, i % CS
            to = (x ^ (k & 2), y ^ (k & 1) * 2) if s < 2 else partner(x, y, c, k)
            pairs.append((i, s * XS * YS * CS + place(*to, c)))
        turns.append(lax.ppermute(first, ("section", "dp"), pairs))
    turns = jnp.concatenate(turns)
    own = jnp.where(gather, at_x // 2 * 2 + at_y // 2, at_x % 2 * 2 + at_y % 2)
    order = [own ^ jnp.where(gather, ROUND[j], j) for j in range(4)]
    got = jnp.stack([lax.dynamic_index_in_dim(turns, j, 0, False) for j in order])

    def run_first():
        outs = end_forward(exchange(product_forward(got, lambda x: x), BLOCKS), tokens)
        return outs[0], outs[3], outs[4]

    def run_target():
        return whole_call(
            functools.partial(post_target, rank),
            "post_target",
            [main],
            [backward(got, lambda x: x), a_turned, member, gain],
            scratch=[store],
        )

    brief = [main] + kept_outs[3:]
    (ahead,) = only(3, run_target, [main])
    got, ahead = lax.optimization_barrier((got, ahead))
    ahead = hop(ahead, [(3, 2)])
    result_0, inverse_0, down_0 = only(0, run_first, brief)
    first = hop(result_0, [(0, 1)])
    back_first, ranks_first = only(2, lambda: sums_of(got), [wide, thin])

    back_late, ranks_late = only(2, lambda: sums_of(exchange(plain(ahead), BLOCKS)), [wide, thin])
    halves, back_first = lax.optimization_barrier((halves, back_first))
    halves = near(halves)
    result_1, frozen_1, raw_1, inverse_1, down_1 = only(
        1, lambda: end_forward(forward(first), first), kept_outs
    )
    second = hop(result_1, [(1, 2)])

    def run_turn():
        result, _, raw, inverse, down, sent = whole_call(
            functools.partial(post_forward_turn, width),
            "post_forward_turn",
            kept_outs + [payload],
            [target, ahead, b_flat, forward(second), second, b_turned, member],
            scratch=[store],
        )
        grad, grad_in = whole_call(
            functools.partial(post_turn, width),
            "post_turn",
            [main, main],
            [backward(exchange(sent, BLOCKS)), back_first, ranks_first, back_late, ranks_late, target, ahead]
            + [result, second, a_turned, member, raw, inverse, gain],
            scratch=[store],
        )
        return result, inverse, down, grad, grad_in

    result_2, inverse_2, down_2, grad_2, grad_in = only(2, run_turn, brief + [main, main])
    grad_1 = hop(grad_in, [(2, 1)])
    grad_1, result_2 = lax.optimization_barrier((grad_1, result_2))
    third = hop(result_2, [(2, 3)])

    def run_back():
        (sent,) = whole_call(
            pre_backward, "pre_backward", [payload], [grad_1, frozen_1, b_flat, member]
        )
        return whole_call(
            functools.partial(post_backward, width),
            "post_backward",
            [main],
            [backward(exchange(sent, BLOCKS)), grad_1, first, a_turned, member, raw_1, inverse_1]
            + [gain],
            scratch=[store],
        )

    def run_last():
        outs = end_forward(forward(third), third)
        return outs[0], outs[3], outs[4]

    (grad_in,) = only(1, run_back, [main])
    grad_0 = hop(grad_in, [(1, 0)])
    result_3, inverse_3, down_3 = only(3, run_last, brief)

    def choose(*values):
        return lax.select_n(section.astype(jnp.int32), *values)

    others = choose(target, grad_1, grad_2, target)
    others, result_3 = lax.optimization_barrier((others, result_3))
    grad, ranks = whole_call(
        ranks_of,
        "ranks_of",
        [main, thin],
        [(section == 0).astype(jnp.int32).reshape(1), grad_0, others, b_flat, member],
        scalars=1,
    )
    (ranks,) = whole_call(
        both_cores,
        "both_cores",
        [((XS * YS, rank, total), BF)],
        [ranks, swap_cores(ranks)],
        flops=1e6,
    )
    saved = [
        [tokens, first, second, third],
        [result_0, result_1, result_2, result_3],
        [inverse_0, inverse_1, inverse_2, inverse_3],
        [down_0, down_1, down_2, down_3],
    ]
    ranks, saved = lax.optimization_barrier((ranks, saved))
    ranks = exchange(ranks, ALONG_XY)
    current, result, inverse, down = [choose(*values) for values in saved]
    (grad_b,) = whole_call(
        outer_up,
        "outer_up",
        [((adapters * rank, cols), F32)],
        [down, grad, member],
        scratch=[store],
    )
    (grad_a,) = whole_call(
        outer_down,
        "outer_down",
        [((adapters * rank, cols), F32)],
        [ranks, current, inverse, gain, member],
        scratch=[store],
    )
    section_out = result.T.reshape(1, micro, rows, cols)
    shape = (1, adapters, rank, cols)
    return section_out, grad_a.reshape(shape), grad_b.reshape(shape)


def solution(mesh):
    in_specs = (
        P(None, None, "dp"),
        P(None, None, "dp"),
        P("section", None, "dp"),
        P("section", "dp"),
        P("section", None, None, "dp"),
        P("section", None, None, "dp"),
        P(),
        P(),
    )
    out_specs = (
        P("section", None, None, "dp"),
        P("section", None, None, "dp"),
        P("section", None, None, "dp"),
    )
    return jax.shard_map(
        on_device, mesh=mesh, in_specs=in_specs, out_specs=out_specs, check_vma=False
    )
```

```python
import functools

import jax
import jax.numpy as jnp
from jax import lax
from jax.experimental import pallas as pl
from jax.experimental.pallas import tpu as pltpu
from jax.sharding import PartitionSpec as P

EPSILON = 1e-06
SCALING = 2.0
XS, YS, CS = 4, 4, 2
BF = jnp.bfloat16
F32 = jnp.float32
VM = pl.BlockSpec(memory_space=pltpu.VMEM)
SM = pl.BlockSpec(memory_space=pltpu.SMEM)
PARAMS = pltpu.CompilerParams(vmem_limit_bytes=24 << 20)


def place(x, y, c):
    return (x * YS + y) * CS + c


def partner(x, y, c, k):
    other = lambda v: (v ^ 1) if c == 0 else ((v + 1) % 4 if v % 2 else (v - 1) % 4)
    return (other(x) if k & 2 else x), (other(y) if k & 1 else y)


APART = [
    [place(x + 2 * i, y + 2 * j, c) for i in range(2) for j in range(2)]
    for x in range(2)
    for y in range(2)
    for c in range(CS)
]
ROUND = (0, 1, 3, 2)
RING = [[group[k] for k in ROUND] for group in APART]
BLOCKS = [
    [place(*partner(x, y, c, k), c) for k in range(4)]
    for x in range(0, XS, 2)
    for y in range(0, YS, 2)
    for c in range(CS)
]
ALONG_XY = [[place(x, y, c) for x in range(XS) for y in range(YS)] for c in range(CS)]
SIBLING = [(i, i ^ 1) for i in range(XS * YS * CS)]


def exchange(chunks, groups):
    return lax.all_to_all(chunks, "dp", 0, 0, axis_index_groups=groups)


def swap_cores(block):
    return lax.ppermute(block, "dp", SIBLING)


def tables_of(seg_ids, live_counts, adapters):
    micro, rows = seg_ids.shape
    labels = jnp.arange(adapters, dtype=jnp.int32)
    member = (seg_ids[:, None, :] == labels[None, :, None]).astype(jnp.int32)
    counts = jnp.sum(member, axis=2)
    before = (labels[:, None] < labels[None, :]).astype(jnp.int32)
    starts = jnp.sum(counts[:, :, None] * before[None], axis=1)
    row_start = jnp.sum(member * starts[:, :, None], axis=1)
    row_limit = jnp.sum(member * jnp.minimum(live_counts, counts)[:, :, None], axis=1)
    live = jnp.arange(rows, dtype=jnp.int32)[None] - row_start < row_limit
    whole = member.astype(F32).transpose(1, 0, 2).reshape(adapters, micro * rows)
    return whole, live.reshape(micro * rows)


def dot(left, right, dims=((1,), (0,))):
    return lax.dot_general(left, right, (dims, ((), ())), preferred_element_type=F32)


def tail_of(ranks, rows):
    high = rows.astype(BF).astype(F32)
    return jnp.concatenate([ranks, high, rows - high], axis=0).astype(BF)


def eight(*rows):
    index = lax.broadcasted_iota(jnp.int32, (8, rows[0].shape[1]), 0)
    total = jnp.zeros(index.shape, F32)
    for at, row in enumerate(rows):
        total = jnp.where(index == at, row, total)
    return total


def extras(chunks, cols, rank):
    total = chunks[0, cols:].astype(F32)
    for j in range(1, chunks.shape[0]):
        total = total + chunks[j, cols:].astype(F32)
    return total[:rank], total[rank : rank + 8] + total[rank + 8 :]


def mains(chunks, cols):
    total = chunks[0, :cols].astype(F32)
    for j in range(1, chunks.shape[0]):
        total = total + chunks[j, :cols].astype(F32)
    return total


def select_rank(parts, member, rank):
    total = None
    for a in range(member.shape[0]):
        part = parts[a * rank : (a + 1) * rank] * member[a : a + 1, :]
        total = part if total is None else total + part
    return total


def spread_rank(values, member, store):
    rank = values.shape[0]
    for a in range(member.shape[0]):
        store[a * rank : (a + 1) * rank] = (values * member[a : a + 1, :]).astype(BF)


def fill(sent, main, tail):
    cols = main.shape[0]
    for j in range(sent.shape[0]):
        sent[j, :cols] = main
        sent[j, cols:] = tail


def column_sum(left, right):
    return jnp.sum(left * right, axis=0, keepdims=True)


def pre_forward(current, gain, a_flat, member, sent):
    rank = a_flat.shape[0] // member.shape[0]
    values = current[...].astype(F32)
    scaled = (values * gain[...]).astype(BF)
    ranks = select_rank(dot(a_flat[...], scaled), member, rank)
    fill(sent, scaled, tail_of(ranks, eight(column_sum(values, values))))


def turn_rows(got, cols, turned):
    @pl.when(pl.program_id(0) == 0)
    def _():
        parts = [got[k, :cols] for k in ROUND]
        turned[...] = jnp.concatenate(parts, axis=0).T


def mid_forward_own(info, got, weight, total, turned):
    cols = weight.shape[-1]
    turn_rows(got, cols, turned)
    for i in range(total.shape[0]):
        total[i] = dot(turned[...], weight[i].reshape(YS * cols, cols))


def mid_forward(info, got, other, weight, total, sent, turned):
    cols = weight.shape[-1]
    rank = got.shape[1] - cols - 16
    turn_rows(other, cols, turned)
    ranks, rows = extras(got, cols, rank)
    ranks_o, rows_o = extras(other, cols, rank)
    tail = tail_of(ranks + ranks_o, rows + rows_o)
    for i in range(sent.shape[0]):
        both = total[i] + dot(turned[...], weight[i].reshape(YS * cols, cols))
        sent[i, :cols] = both.astype(BF).T
        sent[i, cols:] = tail


def finish(width, got, current, b_turned, member, result, frozen, down_raw, inverse, down, store):
    cols, rank = current.shape[0], down.shape[0]
    total = mains(got, cols)
    ranks, rows = extras(got, cols, rank)
    scale = lax.rsqrt(rows[0:1] / width + EPSILON)
    kept = (ranks * scale).astype(BF)
    spread_rank(kept.astype(F32), member, store)
    adapter = dot(b_turned[...], store[...])
    value = (current[...].astype(F32) + total * scale + SCALING * adapter).astype(BF)
    result[...] = value
    frozen[...] = total
    down_raw[...] = ranks
    inverse[...] = scale
    down[...] = kept
    return value, total


def post_forward(width, *refs):
    finish(width, *refs)


def post_forward_turn(width, target, ahead, b_flat, *refs):
    sent = refs[-2]
    member, rank = refs[3], refs[-3].shape[0]
    value, frozen = finish(width, *refs[:-2], refs[-1])
    ranks = select_rank(dot(b_flat[...], value), member, rank)
    values = value.astype(F32)
    early, late = target[...].astype(F32), ahead[...].astype(F32)
    rows = eight(
        column_sum(values, values),
        column_sum(values, late),
        column_sum(early, frozen),
        column_sum(late, frozen),
        column_sum(values, frozen),
    )
    fill(sent, value, tail_of(ranks, rows))


def pre_backward(grad, frozen, b_flat, member, sent):
    rank = b_flat.shape[0] // member.shape[0]
    kept = grad[...]
    ranks = select_rank(dot(b_flat[...], kept), member, rank)
    row = column_sum(kept.astype(F32), frozen[...])
    fill(sent, kept, tail_of(ranks, eight(row)))


def pre_plain(grad, b_flat, member, sent):
    rank = b_flat.shape[0] // member.shape[0]
    kept = grad[...]
    ranks = select_rank(dot(b_flat[...], kept), member, rank)
    fill(sent, kept, tail_of(ranks, jnp.zeros((8, kept.shape[1]), F32)))


def row_product(got, weight):
    chips, cols = weight.shape[1], weight.shape[-1]
    left = [weight[j].reshape(chips * cols, cols) for j in range(XS)]
    right = [got[j, :cols] for j in range(XS)]
    total = dot(jnp.concatenate(left, axis=1), jnp.concatenate(right, axis=0))
    return total.reshape(chips, cols, total.shape[1])


def mid_backward_other(info, got, weight, sent):
    cols = weight.shape[-1]
    main = row_product(got, weight).astype(BF)
    tail = tail_of(*extras(got, cols, got.shape[1] - cols - 16))
    for j in range(sent.shape[0]):
        sent[j, :cols] = main[j]
        sent[j, cols:] = tail


def mid_backward_own(info, got, weight, total):
    total[...] = row_product(got, weight)


def mid_backward(got, total, other, sent):
    cols = total.shape[1]
    rank = got.shape[1] - cols - 16
    ranks, rows = extras(got, cols, rank)
    ranks_o, rows_o = extras(other[:1], cols, rank)
    tail = tail_of(ranks + ranks_o, rows + rows_o)
    for j in range(sent.shape[0]):
        sent[j, :cols] = (total[j] + other[j, :cols].astype(F32)).astype(BF)
        sent[j, cols:] = tail


def add_up(got, total, ranks):
    cols, rank = total.shape[0], ranks.shape[0]
    total[...] = mains(got, cols)
    ranks[...] = extras(got, cols, rank)[0]


def post_target(rank, got, a_turned, member, gain, ahead, store):
    cols = ahead.shape[0]
    ranks, _ = extras(got, cols, rank)
    spread_rank((SCALING * ranks).astype(BF).astype(F32), member, store)
    normed_grad = mains(got, cols) + dot(a_turned[...], store[...])
    ahead[...] = (gain[...] * normed_grad).astype(BF)


def step_back(
    width, grad, back, ranks, row, current, a_turned, member, down_raw, inverse, gain, store
):
    grad_down = (SCALING * ranks).astype(BF).astype(F32)
    spread_rank(grad_down, member, store)
    normed_grad = back + dot(a_turned[...], store[...])
    stat = (row + column_sum(grad_down, down_raw[...])) / width
    scale = inverse[...]
    return (
        grad
        + scale * gain[...] * normed_grad
        - current[...].astype(F32) * (scale * scale * scale * stat)
    ).astype(BF)


def post_backward(
    width, got, grad, current, a_turned, member, down_raw, inverse, gain, grad_in, store
):
    cols, rank = current.shape[0], down_raw.shape[0]
    ranks, rows = extras(got, cols, rank)
    grad_in[...] = step_back(
        width, grad[...].astype(F32), mains(got, cols), ranks, rows[0:1],
        current, a_turned, member, down_raw, inverse, gain, store,
    )


def post_turn(
    width, got, back_first, ranks_first, back_late, ranks_late, target, ahead, result,
    current, a_turned, member, down_raw, inverse, gain, grad, grad_in, store,
):
    cols, rank = current.shape[0], down_raw.shape[0]
    ranks, rows = extras(got, cols, rank)
    scale = lax.rsqrt(rows[0:1] / width + EPSILON)
    least = scale * scale * scale * (rows[1:2] / width)
    fresh = (
        target[...].astype(F32)
        + scale * ahead[...].astype(F32)
        - least * result[...].astype(F32)
    )
    kept = fresh.astype(BF)
    grad[...] = kept
    grad_in[...] = step_back(
        width,
        kept.astype(F32),
        back_first[...] + scale * back_late[...] - least * mains(got, cols),
        ranks_first[...] + scale * ranks_late[...] - least * ranks,
        rows[2:3] + scale * rows[3:4] - least * rows[4:5],
        current, a_turned, member, down_raw, inverse, gain, store,
    )


def ranks_of(flag, received, others, b_flat, member, grad, ranks):
    kept = jnp.where(flag[0] > 0, received[...].astype(F32), others[...].astype(F32)).astype(BF)
    grad[...] = kept
    ranks[...] = select_rank(dot(b_flat[...], kept), member, ranks.shape[0])


def both_cores(ranks, other, sent):
    both = (ranks[...] + other[...]).astype(BF)
    for j in range(sent.shape[0]):
        sent[j] = both


def outer_up(down, grad, member, grad_b, store):
    spread_rank(SCALING * down[...].astype(F32), member, store)
    grad_b[...] = dot(store[...], grad[...], ((1,), (1,)))


def outer_down(got, current, inverse, gain, member, grad_a, store):
    ranks = got[0].astype(F32)
    for j in range(1, got.shape[0]):
        ranks = ranks + got[j].astype(F32)
    spread_rank((SCALING * ranks).astype(BF).astype(F32), member, store)
    normed = (current[...].astype(F32) * inverse[...] * gain[...]).astype(BF)
    grad_a[...] = dot(store[...], normed, ((1,), (1,)))


def reorder(weight, block):
    block[0, 0, 0] = weight[0, 0, :, 0]


def bring(block, kept, sem):
    copy = pltpu.make_async_copy(block, kept, sem)
    copy.start()
    copy.wait()


def cost(flops, arrays):
    return pl.CostEstimate(
        flops=int(flops),
        bytes_accessed=sum(x.size * x.dtype.itemsize for x in arrays),
        transcendentals=0,
    )


def held(value):
    return pltpu.with_memory_space_constraint(value, pltpu.VMEM)


def whole_call(body, name, outs, ins, scratch=(), flops=4e8, scalars=0):
    return pl.pallas_call(
        body,
        out_shape=[jax.ShapeDtypeStruct(s, d) for s, d in outs],
        in_specs=[SM] * scalars + [VM] * (len(ins) - scalars),
        out_specs=[VM] * len(outs),
        scratch_shapes=list(scratch),
        compiler_params=PARAMS,
        cost_estimate=cost(flops, ins),
        name=name,
    )(*ins)


def on_device(
    tokens_in, cotangent, base_weight, norm_gain, adapter_a, adapter_b, seg_ids, live_counts
):
    section = lax.axis_index("section")
    at = lax.axis_index("dp")
    at_x, at_y, core = at // (YS * CS), (at // CS) % YS, at % CS
    micro, rows, cols = tokens_in.shape
    total = micro * rows
    adapters, rank = adapter_a.shape[1:3]
    width = base_weight.shape[1]
    tall = cols + rank + 16
    gain = norm_gain[0].astype(F32)[:, None]
    a_flat = adapter_a[0].reshape(adapters * rank, cols)
    b_flat = adapter_b[0].reshape(adapters * rank, cols)
    a_turned, b_turned = a_flat.T, b_flat.T
    member, live = tables_of(seg_ids, live_counts, adapters)
    gain, a_turned, b_turned = lax.optimization_barrier((gain, a_turned, b_turned))
    info = core.astype(jnp.int32).reshape(1)
    store = pltpu.VMEM((adapters * rank, total), BF)
    payload = ((XS, tall, total), BF)
    main = ((cols, total), BF)
    wide = ((cols, total), F32)
    thin = ((rank, total), F32)
    kept_outs = [main, wide, thin, ((1, total), F32), ((rank, total), BF)]

    pair = CS * cols
    block = pl.pallas_call(
        reorder,
        grid=(2, 2, 2),
        in_specs=[
            pl.BlockSpec((1, 1, 2, 1, pair, cols), lambda p, q, i: (i, p, 0, q, 0, 0)),
        ],
        out_specs=pl.BlockSpec((1, 1, 1, 2, pair, cols), lambda p, q, i: (p, q, i, 0, 0, 0)),
        out_shape=jax.ShapeDtypeStruct((2, 2, 2, 2, pair, cols), BF),
        compiler_params=PARAMS,
        name="reorder",
    )(base_weight[0].reshape(2, 2, 2, 2, pair, cols))
    block = exchange(block.reshape(XS, width // XS, cols), BLOCKS)
    halves = block.reshape(XS, YS, CS, cols, cols)
    tokens = tokens_in.reshape(total, cols).T
    target = jnp.where(live[None, :], cotangent.reshape(total, cols).T, jnp.zeros((), BF))

    def mid_call(body, name, steps, specs, ins, out, out_rows, flops, scratch=()):
        return pl.pallas_call(
            body,
            grid_spec=pltpu.PrefetchScalarGridSpec(
                num_scalar_prefetch=1,
                grid=(steps,),
                in_specs=specs,
                out_specs=pl.BlockSpec((XS // steps,) + out_rows, lambda i, c: (i, 0, 0)),
                scratch_shapes=list(scratch),
            ),
            out_shape=jax.ShapeDtypeStruct((XS,) + out_rows, out),
            compiler_params=PARAMS,
            cost_estimate=cost(flops, ins),
            name=name,
        )(info, *ins)

    tall_full = pl.BlockSpec((XS, tall, total), lambda i, c: (0, 0, 0))

    def start_forward(current, out=payload):
        (sent,) = whole_call(pre_forward, "pre_forward", [out], [current, gain, a_flat, member])
        return sent

    def near(value):
        return pl.pallas_call(
            bring,
            out_shape=pltpu.VMEM(value.shape, value.dtype),
            in_specs=[pl.BlockSpec(memory_space=pl.ANY)],
            out_specs=VM,
            scratch_shapes=[pltpu.SemaphoreType.DMA],
            compiler_params=PARAMS,
            cost_estimate=cost(8e8, [value]),
            name="bring",
        )(value)

    def product_forward(got, held=held):
        shape = (2, YS, 1, cols, cols)
        other = swap_cores(got)
        own = mid_call(
            mid_forward_own,
            "mid_forward_own",
            2,
            [tall_full, pl.BlockSpec(shape, lambda i, c: (i, 0, c[0], 0, 0))],
            [got, held(halves)],
            F32,
            (total, cols),
            8e8,
            [pltpu.VMEM((total, YS * cols), BF)],
        )
        return mid_call(
            mid_forward,
            "mid_forward",
            2,
            [
                tall_full,
                tall_full,
                pl.BlockSpec(shape, lambda i, c: (i, 0, 1 - c[0], 0, 0)),
                pl.BlockSpec((2, total, cols), lambda i, c: (i, 0, 0)),
            ],
            [got, other, held(halves), own],
            BF,
            (tall, total),
            8e8,
            [pltpu.VMEM((total, YS * cols), BF)],
        )

    def end_forward(got, current):
        return whole_call(
            functools.partial(post_forward, width),
            "post_forward",
            kept_outs,
            [got, current, b_turned, member],
            scratch=[store],
        )

    def forward(current):
        sent = start_forward(current, ((1, tall, total), BF))
        got = lax.all_gather(sent, "dp", axis_index_groups=RING, axis=0, tiled=True)
        return exchange(product_forward(got), BLOCKS)

    def product_backward(got, held=held):
        shape = (XS, 2, 1, cols, cols)
        other = mid_call(
            mid_backward_other,
            "mid_backward_other",
            2,
            [tall_full, pl.BlockSpec(shape, lambda i, c: (0, i, 1 - c[0], 0, 0))],
            [got, held(halves)],
            BF,
            (tall, total),
            8e8,
        )
        own = mid_call(
            mid_backward_own,
            "mid_backward_own",
            2,
            [tall_full, pl.BlockSpec(shape, lambda i, c: (0, i, c[0], 0, 0))],
            [got, held(halves)],
            F32,
            (cols, total),
            8e8,
        )
        (sent,) = whole_call(
            mid_backward, "mid_backward", [payload], [got, own, swap_cores(other)], flops=1e6
        )
        return sent

    def backward(got, held=held):
        return exchange(product_backward(got, held), APART)

    def plain(vector, out=payload):
        return whole_call(pre_plain, "pre_plain", [out], [vector, b_flat, member])[0]

    def sums_of(got):
        return whole_call(add_up, "add_up", [wide, thin], [backward(got, lambda x: x)])

    def zeros(*kinds):
        return [jnp.zeros(*kind) for kind in kinds]

    def hop(value, pairs):
        return lax.ppermute(value, "section", pairs)

    def only(place, work, outs):
        return lax.cond(section == place, lambda: tuple(work()), lambda: tuple(zeros(*outs)))

    single = ((1, tall, total), BF)
    gather = section < 2
    first = jnp.where(gather, start_forward(tokens, single), plain(target, single))
    turns = [first]
    for k in range(1, 4):
        pairs = []
        for i in range(4 * XS * YS * CS):
            s, x, y, c = i // (XS * YS * CS), i // (YS * CS) % XS, i // CS % YS, i % CS
            to = (x ^ (k & 2), y ^ (k & 1) * 2) if s < 2 else partner(x, y, c, k)
            pairs.append((i, s * XS * YS * CS + place(*to, c)))
        turns.append(lax.ppermute(first, ("section", "dp"), pairs))
    turns = jnp.concatenate(turns)
    own = jnp.where(gather, at_x // 2 * 2 + at_y // 2, at_x % 2 * 2 + at_y % 2)
    order = [own ^ jnp.where(gather, ROUND[j], j) for j in range(4)]
    got = jnp.stack([lax.dynamic_index_in_dim(turns, j, 0, False) for j in order])

    def run_first():
        outs = end_forward(exchange(product_forward(got, lambda x: x), BLOCKS), tokens)
        return outs[0], outs[3], outs[4]

    def run_target():
        return whole_call(
            functools.partial(post_target, rank),
            "post_target",
            [main],
            [backward(got, lambda x: x), a_turned, member, gain],
            scratch=[store],
        )

    brief = [main] + kept_outs[3:]
    (ahead,) = only(3, run_target, [main])
    ahead = hop(ahead, [(3, 2)])
    back_first, ranks_first = only(2, lambda: sums_of(got), [wide, thin])
    got, back_first = lax.optimization_barrier((got, back_first))
    result_0, inverse_0, down_0 = only(0, run_first, brief)
    first = hop(result_0, [(0, 1)])

    back_late, ranks_late = only(2, lambda: sums_of(exchange(plain(ahead), BLOCKS)), [wide, thin])
    halves, back_first = lax.optimization_barrier((halves, back_first))
    halves = near(halves)
    result_1, frozen_1, raw_1, inverse_1, down_1 = only(
        1, lambda: end_forward(forward(first), first), kept_outs
    )
    second = hop(result_1, [(1, 2)])

    def run_turn():
        result, _, raw, inverse, down, sent = whole_call(
            functools.partial(post_forward_turn, width),
            "post_forward_turn",
            kept_outs + [payload],
            [target, ahead, b_flat, forward(second), second, b_turned, member],
            scratch=[store],
        )
        grad, grad_in = whole_call(
            functools.partial(post_turn, width),
            "post_turn",
            [main, main],
            [backward(exchange(sent, BLOCKS)), back_first, ranks_first, back_late, ranks_late, target, ahead]
            + [result, second, a_turned, member, raw, inverse, gain],
            scratch=[store],
        )
        return result, inverse, down, grad, grad_in

    result_2, inverse_2, down_2, grad_2, grad_in = only(2, run_turn, brief + [main, main])
    grad_1 = hop(grad_in, [(2, 1)])
    grad_1, result_2 = lax.optimization_barrier((grad_1, result_2))
    third = hop(result_2, [(2, 3)])

    def run_back():
        (sent,) = whole_call(
            pre_backward, "pre_backward", [payload], [grad_1, frozen_1, b_flat, member]
        )
        return whole_call(
            functools.partial(post_backward, width),
            "post_backward",
            [main],
            [backward(exchange(sent, BLOCKS)), grad_1, first, a_turned, member, raw_1, inverse_1]
            + [gain],
            scratch=[store],
        )

    def run_last():
        outs = end_forward(forward(third), third)
        return outs[0], outs[3], outs[4]

    (grad_in,) = only(1, run_back, [main])
    grad_0 = hop(grad_in, [(1, 0)])
    result_3, inverse_3, down_3 = only(3, run_last, brief)

    def choose(*values):
        return lax.select_n(section.astype(jnp.int32), *values)

    others = choose(target, grad_1, grad_2, target)
    others, result_3 = lax.optimization_barrier((others, result_3))
    grad, ranks = whole_call(
        ranks_of,
        "ranks_of",
        [main, thin],
        [(section == 0).astype(jnp.int32).reshape(1), grad_0, others, b_flat, member],
        scalars=1,
    )
    (ranks,) = whole_call(
        both_cores,
        "both_cores",
        [((XS * YS, rank, total), BF)],
        [ranks, swap_cores(ranks)],
        flops=1e6,
    )
    saved = [
        [tokens, first, second, third],
        [result_0, result_1, result_2, result_3],
        [inverse_0, inverse_1, inverse_2, inverse_3],
        [down_0, down_1, down_2, down_3],
    ]
    ranks, saved = lax.optimization_barrier((ranks, saved))
    ranks = exchange(ranks, ALONG_XY)
    current, result, inverse, down = [choose(*values) for values in saved]
    (grad_b,) = whole_call(
        outer_up,
        "outer_up",
        [((adapters * rank, cols), F32)],
        [down, grad, member],
        scratch=[store],
    )
    (grad_a,) = whole_call(
        outer_down,
        "outer_down",
        [((adapters * rank, cols), F32)],
        [ranks, current, inverse, gain, member],
        scratch=[store],
    )
    section_out = result.T.reshape(1, micro, rows, cols)
    shape = (1, adapters, rank, cols)
    return section_out, grad_a.reshape(shape), grad_b.reshape(shape)


def solution(mesh):
    in_specs = (
        P(None, None, "dp"),
        P(None, None, "dp"),
        P("section", None, "dp"),
        P("section", "dp"),
        P("section", None, None, "dp"),
        P("section", None, None, "dp"),
        P(),
        P(),
    )
    out_specs = (
        P("section", None, None, "dp"),
        P("section", None, None, "dp"),
        P("section", None, None, "dp"),
    )
    return jax.shard_map(
        on_device, mesh=mesh, in_specs=in_specs, out_specs=out_specs, check_vma=False
    )
```
